256 devices in a mesh: head: 8 (over y, core), ctx: 32 (over x, z).
Axes of the slice: x: 4, y: 4, z: 8, core: 2. Of those that a mesh axis runs over, the one named last changes fastest.
Arguments:
- queries: bfloat16 [12288, 5120], P('ctx', 'head'), may hold values from -150 to 150
- keys: bfloat16 [12288, 5120], P('ctx', 'head'), may hold values from -21.1 to 21.1
- values: bfloat16 [12288, 5120], P('ctx', 'head'), may hold values from -6 to 6
- grad_out: bfloat16 [12288, 5120], P('ctx', 'head'), may hold values from -192 to 192
- key_tiles: int32 [32, 6], replicated, may hold values from -1 to 31, as said below
- tile_slot: int32 [32], replicated, may hold values from 0 to 31, as said below
Outputs:
- grad_queries: bfloat16 [32, 384, 5120], P('ctx', 'head')
- grad_keys: bfloat16 [32, 384, 5120], P('ctx', 'head')
- grad_values: bfloat16 [32, 384, 5120], P('ctx', 'head')
The draws below stay inside these ranges and needn't reach their ends.
Inputs may be any that keep to these rules, and one draw needn't show every extreme that they name: tile_slot[t] = t for every tile t (each storage block holds one tile). `key_tiles`: row t lists in increasing order tile t and other tiles within 3 of t, distinct; where all 7 tiles around t exist, exactly one tile other than t is left out, else all existing ones are listed and -1 fills the remaining entries.
All inputs are finite; a program needn't handle non-finite values.
Results may differ from the reference program's by a relative error of at most 0.01.
Values may be sent and summed in bfloat16 or wider, within the bound.
A program may use at most 128 MiB of HBM per device.

```python
import math
import jax
import jax.numpy as jnp
from jax import lax

DH = 128
TILE = 384
REACH = 3
LIST = 6
TILES_DEV = 1
HEADS = 40
TILES = 32
TOKENS = 12288


def shared_base(key):
    base = jax.random.truncated_normal(key, -6.0, 6.0, (TOKENS, HEADS * DH), jnp.float32)
    return base


def draw_keys(key, part):
    base = shared_base(key)
    key = jax.random.fold_in(key, 3)
    scale_key = jax.random.fold_in(key, 0)
    row_scale = jnp.exp(jax.random.uniform(scale_key, (TOKENS, 1), jnp.float32, math.log(0.35), math.log(3.5)))
    result = base * row_scale
    return result.astype(jnp.bfloat16)


def draw_queries(key, part):
    key = jax.random.fold_in(key, 4)
    scale_key, other_key = jax.random.split(key)
    row_scale = jnp.exp(jax.random.uniform(scale_key, (TOKENS, 1), jnp.float32, math.log(0.03), math.log(0.3)))
    fresh = jax.random.truncated_normal(other_key, -6.0, 6.0, (TOKENS, HEADS * DH), jnp.float32)
    result = fresh * row_scale
    return result.astype(jnp.bfloat16)


def draw_key_tiles(key, part):
    key = jax.random.fold_in(key, 5)
    width = 2 * REACH + 1
    tiles = jnp.arange(TILES, dtype=jnp.int32)[:, None]
    offsets = jnp.arange(width, dtype=jnp.int32)[None, :]
    candidates = tiles + offsets - REACH
    inside = (candidates >= 0) & (candidates < TILES)
    complete = jnp.all(inside, axis=1, keepdims=True)
    picked = jax.random.randint(key, (TILES, 1), 0, 2 * REACH, jnp.int32)
    dropped = picked + (picked >= REACH).astype(jnp.int32)
    retained = inside & jnp.logical_not(complete & (offsets == dropped))
    ranking = jnp.where(retained, offsets, offsets + width)
    order = jnp.argsort(ranking, axis=1, stable=True)
    listed = jnp.take_along_axis(jnp.where(retained, candidates, -1), order, axis=1)
    return listed[:, :LIST].astype(jnp.int32)


def draw_tile_slot(key, part):
    key = jax.random.fold_in(key, 7)
    blocks = TILES // TILES_DEV
    orders = jax.vmap(lambda single: jax.random.permutation(single, TILES_DEV))(jax.random.split(key, blocks))
    slots = jnp.arange(blocks, dtype=jnp.int32)[:, None] * TILES_DEV + orders.astype(jnp.int32)
    return slots.reshape(TILES).astype(jnp.int32)


def level_of(stream_key, dims, cuts, low, largest):
    loudness = 1.0
    for dim, shards_of in cuts:
        draws = jax.random.uniform(jax.random.fold_in(jax.random.fold_in(stream_key, 6), dim), (shards_of,), jnp.float32, low / len(cuts), largest / len(cuts))
        loudness = loudness * jnp.repeat(jnp.exp(draws), dims[dim] // shards_of).reshape((-1,) + (1,) * (len(dims) - 1 - dim))
    return loudness


def gaussian(own_key, shape, scale, reach, shards=(), kind=jnp.bfloat16):
    gain = level_of(own_key, shape, shards, -0.22, 0.18) if shards else 1.0
    values = jax.random.normal(own_key, shape, jnp.float32) * scale * gain
    return jnp.minimum(jnp.maximum(values, -reach), reach).astype(kind)


def setup_inputs(seed: int = 0) -> dict:
    seeds = jax.random.split(jax.random.key(seed), 7)
    queries = draw_queries(jax.random.fold_in(seeds[6], 71), 0)
    keys = draw_keys(jax.random.fold_in(seeds[6], 71), 0)
    values = gaussian(seeds[2], (TOKENS, HEADS * DH), 1.0, 6.0, ((0, 32), (1, 8)))
    grad_out = gaussian(seeds[3], (TOKENS, HEADS * DH), 32.0, 192.0, ((0, 32), (1, 8)))
    key_tiles = draw_key_tiles(jax.random.fold_in(seeds[6], 71), 0)
    tile_slot = draw_tile_slot(jax.random.fold_in(seeds[6], 71), 0)
    return dict(queries=queries, keys=keys, values=values, grad_out=grad_out, key_tiles=key_tiles, tile_slot=tile_slot)


def rounded(value):
    return lax.optimization_barrier(value.astype(jnp.bfloat16)).astype(jnp.float32)


def reference(queries, keys, values, grad_out, key_tiles, tile_slot):
    scale = DH ** -0.5
    shape_four = (TILES, TILE, HEADS, DH)
    query_all = queries.reshape(shape_four)
    key_all = keys.reshape(shape_four)
    value_all = values.reshape(shape_four)
    grad_all = grad_out.reshape(shape_four)
    highest = lax.Precision.HIGHEST

    def visit(carry, tile_index):
        key_acc, value_acc = carry
        slot = tile_slot[tile_index]
        listed = key_tiles[tile_index]
        usable = listed >= 0
        key_slots = tile_slot[jnp.maximum(listed, 0)]
        query_block = query_all[slot].astype(jnp.float32)
        grad_block = grad_all[slot].astype(jnp.float32)
        key_block = key_all[key_slots].astype(jnp.float32)
        value_block = value_all[key_slots].astype(jnp.float32)
        scores = jnp.einsum("qhd,jkhd->hqjk", query_block, key_block, precision=highest) * scale
        scores = jnp.where(usable[None, None, :, None], scores, -1e30)
        summit = jnp.max(scores, axis=(2, 3), keepdims=True)
        expon = jnp.exp(scores - summit)
        probs = expon / jnp.sum(expon, axis=(2, 3), keepdims=True)
        dprobs = jnp.einsum("qhd,jkhd->hqjk", grad_block, value_block, precision=highest)
        delta = jnp.sum(probs * dprobs, axis=(2, 3), keepdims=True)
        dscores = rounded(probs * (dprobs - delta))
        probs_low = rounded(probs)
        grad_query = jnp.einsum("hqjk,jkhd->qhd", dscores, key_block, precision=highest) * scale
        weight = usable.astype(jnp.float32)[:, None, None, None]
        key_part = jnp.einsum("hqjk,qhd->jkhd", dscores, query_block, precision=highest) * scale * weight
        value_part = jnp.einsum("hqjk,qhd->jkhd", probs_low, grad_block, precision=highest) * weight
        key_acc = key_acc.at[key_slots].add(key_part)
        value_acc = value_acc.at[key_slots].add(value_part)
        return (key_acc, value_acc), grad_query.astype(jnp.bfloat16)

    start = (jnp.zeros(shape_four, jnp.float32), jnp.zeros(shape_four, jnp.float32))
    (key_acc, value_acc), grad_tiles = lax.scan(visit, start, jnp.arange(TILES, dtype=jnp.int32))
    grad_slots = jnp.zeros(shape_four, jnp.bfloat16).at[tile_slot].set(grad_tiles)
    final_shape = (TILES, TILE, HEADS * DH)
    return (grad_slots.reshape(final_shape),
            key_acc.astype(jnp.bfloat16).reshape(final_shape),
            value_acc.astype(jnp.bfloat16).reshape(final_shape))
```

```python
import functools
import math

import jax
import jax.numpy as jnp
from jax import lax
from jax.experimental import pallas as pl
from jax.experimental.pallas import tpu as pltpu
from jax.sharding import PartitionSpec as P

DH = 128
REACH = 3
SPAN = 2 * REACH + 1
LOW = -1e30
MESH = pl.DeviceIdType.MESH
NT = (((1,), (1,)), ((), ()))

LAG_A = 2
LAG_C = 3
LAG_B = 3


def kernel(
    n_ctx, n_head, heads, tile,
    tiles_ref, q_hbm, k_hbm, v_hbm, g_hbm,
    dq_hbm, dk_hbm, dv_hbm,
    win, kv, expon, dprob, summit, stat_out, stat_in, res_out, res_in, bias,
    part, hop_out, hop_in, block_q, block_k, block_v,
    load_sem, kv_sem, win_send, win_recv, stat_send, stat_recv, res_send, res_recv,
    hop_send, hop_recv, out_send, out_recv, own_sem,
):
    me = lax.axis_index("ctx")
    lane = lax.axis_index("head")
    rows = tile // n_head
    thirds = tile // 128
    scale = DH ** -0.5
    log_scale = scale * math.log2(math.e)

    def at(offset):
        return lax.rem(me + offset + n_ctx, n_ctx)

    barrier = pltpu.get_barrier_semaphore()
    for offset in range(-REACH, REACH + 1):
        if offset != 0:
            pl.semaphore_signal(
                barrier, inc=1, device_id={"ctx": at(offset)}, device_id_type=MESH
            )
    for shift in range(1, n_head):
        pl.semaphore_signal(
            barrier, inc=1, device_id={"head": lax.rem(lane + shift, n_head)},
            device_id_type=MESH,
        )

    def columns(h):
        return pl.ds(pl.multiple_of(h * DH, DH), DH)

    def own_loads(h):
        return [
            pltpu.make_async_copy(q_hbm.at[:, columns(h)], win.at[REACH, h, 0], load_sem.at[h, 0]),
            pltpu.make_async_copy(g_hbm.at[:, columns(h)], win.at[REACH, h, 1], load_sem.at[h, 1]),
        ]

    def kv_loads(h):
        return [
            pltpu.make_async_copy(k_hbm.at[:, columns(h)], kv.at[h, 0], kv_sem.at[h, 0]),
            pltpu.make_async_copy(v_hbm.at[:, columns(h)], kv.at[h, 1], kv_sem.at[h, 1]),
        ]

    @pl.loop(0, heads)
    def _(h):
        for copy in own_loads(h) + kv_loads(h):
            copy.start()

    for p in range(SPAN):
        other = at(p - REACH)
        mine = jnp.zeros((), jnp.bool_)
        theirs = jnp.zeros((), jnp.bool_)
        for j in range(tiles_ref.shape[1]):
            mine = jnp.logical_or(mine, tiles_ref[me, j] == other)
            theirs = jnp.logical_or(theirs, tiles_ref[other, j] == me)
        bias[0, p] = jnp.where(mine, 0.0, LOW)
        bias[1, p] = jnp.where(theirs, 0.0, LOW)

    pl.semaphore_wait(barrier, 2 * REACH + n_head - 1)

    def relay(direction, distance, h):
        step = -1 if direction == 0 else 1
        source = REACH + step * distance
        return pltpu.make_async_remote_copy(
            src_ref=win.at[source, h],
            dst_ref=win.at[source + step, h],
            send_sem=win_send.at[direction, distance, h],
            recv_sem=win_recv.at[direction, distance, h],
            device_id={"ctx": at(-step)},
            device_id_type=MESH,
        )

    def hop(direction, distance, h):
        return pltpu.make_async_remote_copy(
            src_ref=hop_out.at[direction, distance, h],
            dst_ref=hop_in.at[direction, distance, h],
            send_sem=hop_send.at[direction, distance, h],
            recv_sem=hop_recv.at[direction, distance, h],
            device_id={"ctx": at(-1 if direction == 0 else 1)},
            device_id_type=MESH,
        )

    def stat_copy(p, h):
        return pltpu.make_async_remote_copy(
            src_ref=stat_out.at[h, p],
            dst_ref=stat_in.at[h, 2 * REACH - p],
            send_sem=stat_send.at[h, p],
            recv_sem=stat_recv.at[h, 2 * REACH - p],
            device_id={"ctx": at(p - REACH)},
            device_id_type=MESH,
        )

    def res_copy(p, h):
        return pltpu.make_async_remote_copy(
            src_ref=res_out.at[h],
            dst_ref=res_in.at[h, 2 * REACH - p],
            send_sem=res_send.at[h, p],
            recv_sem=res_recv.at[h, 2 * REACH - p],
            device_id={"ctx": at(p - REACH)},
            device_id_type=MESH,
        )

    def spread(block, target, kind, h):
        place = columns(lane * heads + h)
        pltpu.make_async_copy(
            block.at[h, pl.ds(pl.multiple_of(lane * rows, 16), rows), :],
            target.at[0, :, place],
            own_sem.at[kind, h],
        ).start()

        @pl.loop(1, n_head)
        def _(shift):
            peer = lax.rem(lane + shift, n_head)
            pltpu.make_async_remote_copy(
                src_ref=block.at[h, pl.ds(pl.multiple_of(peer * rows, 16), rows), :],
                dst_ref=target.at[0, :, place],
                send_sem=out_send.at[kind],
                recv_sem=out_recv.at[kind],
                device_id={"head": peer},
                device_id_type=MESH,
            ).start()

    def wide(ref, start):
        return jnp.concatenate([ref[start + j : start + j + 1, :] for j in range(thirds)], axis=1)

    def first_pass(h):
        slot = lax.rem(h, 2)
        for copy in kv_loads(h):
            copy.wait()

        @pl.loop(0, SPAN)
        def _(p):
            scores = lax.dot_general(
                kv[h, 0], win[p, h, 0], NT, preferred_element_type=jnp.float32
            ) * log_scale
            top = jnp.max(scores, axis=0, keepdims=True)
            weights = jnp.exp2(scores - top)
            total = jnp.sum(weights, axis=0, keepdims=True)
            dp = lax.dot_general(kv[h, 1], win[p, h, 1], NT, preferred_element_type=jnp.float32)
            mean = jnp.sum(weights * dp, axis=0, keepdims=True) / total
            expon[slot, p] = weights
            dprob[slot, p] = dp
            summit[slot, p] = top
            level = top + jnp.log2(total)
            for j in range(thirds):
                stat_out[h, p, j : j + 1, :] = level[:, j * 128 : (j + 1) * 128]
                stat_out[h, p, thirds + j : thirds + j + 1, :] = mean[:, j * 128 : (j + 1) * 128]

            @pl.when(p != REACH)
            def _():
                stat_copy(p, h).start()

    def combine(h):
        levels = []
        for p in range(SPAN):
            if p != REACH:
                stat_copy(2 * REACH - p, h).wait_recv()
            source = stat_out if p == REACH else stat_in
            levels.append(source[h, p, 0:thirds, :] + bias[0, p])
        top = functools.reduce(jnp.maximum, levels)
        total = jnp.zeros_like(top)
        delta = jnp.zeros_like(top)
        for p in range(SPAN):
            source = stat_out if p == REACH else stat_in
            weight = jnp.exp2(levels[p] - top)
            total = total + weight
            delta = delta + weight * source[h, p, thirds : 2 * thirds, :]
        level = top + jnp.log2(total)
        delta = delta / total
        res_out[h, 0:thirds, :] = level
        res_out[h, thirds : 2 * thirds, :] = delta
        res_in[h, REACH, 0:thirds, :] = level
        res_in[h, REACH, thirds : 2 * thirds, :] = delta
        for p in range(SPAN):
            if p != REACH:
                res_copy(p, h).start()

    def second_pass(h):
        slot = lax.rem(h, 2)
        keys_turned = kv[h, 0].T

        def body(p, carry):
            dk, dv = carry

            @pl.when(p != REACH)
            def _():
                res_copy(2 * REACH - p, h).wait_recv()

            result = res_in.at[h, p]
            factor = jnp.exp2(summit[slot, p] + bias[1, p] - wide(result, 0))
            delta = wide(result, thirds)
            probs = expon[slot, p] * factor
            dscores = (probs * (dprob[slot, p] - delta)).astype(jnp.bfloat16)
            dv = dv + jnp.dot(
                probs.astype(jnp.bfloat16), win[p, h, 1], preferred_element_type=jnp.float32
            )
            dk = dk + jnp.dot(dscores, win[p, h, 0], preferred_element_type=jnp.float32)
            part[h, p] = (
                jnp.dot(keys_turned, dscores, preferred_element_type=jnp.float32) * scale
            )
            return dk, dv

        start = (jnp.zeros((tile, DH), jnp.float32), jnp.zeros((tile, DH), jnp.float32))
        dk, dv = lax.fori_loop(0, SPAN, body, start)
        for direction, p in ((0, 0), (1, 2 * REACH)):
            hop_out[direction, 0, h] = part[h, p].astype(jnp.bfloat16)
            hop(direction, 0, h).start()
        block_k[h] = (dk * scale).astype(jnp.bfloat16)
        block_v[h] = dv.astype(jnp.bfloat16)
        spread(block_k, dk_hbm, 1, h)
        spread(block_v, dv_hbm, 2, h)

    def pass_on(distance, h):
        for direction, p in ((0, distance), (1, 2 * REACH - distance)):
            hop(direction, distance - 1, h).wait_recv()
            hop_out[direction, distance, h] = (
                part[h, p] + hop_in[direction, distance - 1, h].astype(jnp.float32)
            ).astype(jnp.bfloat16)
            hop(direction, distance, h).start()

    def finish(h):
        total = part[h, REACH]
        for direction in range(2):
            hop(direction, REACH - 1, h).wait_recv()
            total = total + hop_in[direction, REACH - 1, h].astype(jnp.float32)
        block_q[h] = total.T.astype(jnp.bfloat16)
        spread(block_q, dq_hbm, 0, h)

    def send_own(h):
        for copy in own_loads(h):
            copy.wait()
        for direction in range(2):
            relay(direction, 0, h).start()

    send_own(0)

    def during(lag, s, action):
        @pl.when(jnp.logical_and(s >= lag, s < heads + lag))
        def _():
            action(s - lag)

    def forward(distance, h):
        for direction in range(2):
            relay(direction, distance - 1, h).wait_recv()
            if distance < REACH:
                relay(direction, distance, h).start()

    @pl.loop(0, heads + LAG_B + REACH)
    def _(s):
        @pl.when(s < heads - 1)
        def _():
            send_own(s + 1)

        during(0, s, functools.partial(forward, 1))
        during(1, s, functools.partial(forward, 2))
        during(LAG_B + 1, s, functools.partial(pass_on, 1))
        during(LAG_B + 2, s, functools.partial(pass_on, 2))
        during(LAG_B + 3, s, finish)
        during(LAG_C, s, combine)
        during(2, s, functools.partial(forward, 3))
        during(LAG_A, s, first_pass)
        during(LAG_B, s, second_pass)

    @pl.loop(0, heads)
    def _(h):
        for direction in range(2):
            for distance in range(REACH):
                relay(direction, distance, h).wait_send()
                hop(direction, distance, h).wait_send()
        for p in range(SPAN):
            if p != REACH:
                stat_copy(p, h).wait_send()
                res_copy(p, h).wait_send()
        for kind, (block, target) in enumerate(
            ((block_q, dq_hbm), (block_k, dk_hbm), (block_v, dv_hbm))
        ):
            pltpu.make_async_copy(
                block.at[h, pl.ds(pl.multiple_of(lane * rows, 16), rows), :],
                target.at[0, :, columns(lane * heads + h)],
                own_sem.at[kind, h],
            ).wait()

    for kind, target in enumerate((dq_hbm, dk_hbm, dv_hbm)):
        others = target.at[0, :, pl.ds(0, (n_head - 1) * heads * DH)]
        pltpu.make_async_copy(others, others, out_send.at[kind]).wait()
        pltpu.make_async_copy(others, others, out_recv.at[kind]).wait()


def shards(queries, keys, values, grad_out, key_tiles, tile_slot):
    tile, width = queries.shape
    heads = width // DH
    n_ctx = lax.axis_size("ctx")
    n_head = lax.axis_size("head")
    rows = tile // n_head
    bf16, f32 = jnp.bfloat16, jnp.float32
    dma = pltpu.SemaphoreType.DMA
    out = jax.ShapeDtypeStruct((1, rows, n_head * width), bf16)
    pairs = heads * SPAN * tile * tile
    return pl.pallas_call(
        functools.partial(kernel, n_ctx, n_head, heads, tile),
        out_shape=(out, out, out),
        in_specs=[pl.BlockSpec(memory_space=pltpu.SMEM)] + [pl.BlockSpec(memory_space=pl.ANY)] * 4,
        out_specs=tuple([pl.BlockSpec(memory_space=pl.ANY)] * 3),
        scratch_shapes=[
            pltpu.VMEM((SPAN, heads, 2, tile, DH), bf16),
            pltpu.VMEM((heads, 2, tile, DH), bf16),
            pltpu.VMEM((2, SPAN, tile, tile), f32),
            pltpu.VMEM((2, SPAN, tile, tile), f32),
            pltpu.VMEM((2, SPAN, 1, tile), f32),
            pltpu.VMEM((heads, SPAN, 8, 128), f32),
            pltpu.VMEM((heads, SPAN, 8, 128), f32),
            pltpu.VMEM((heads, 8, 128), f32),
            pltpu.VMEM((heads, SPAN, 8, 128), f32),
            pltpu.SMEM((2, SPAN), f32),
            pltpu.VMEM((heads, SPAN, DH, tile), f32),
            pltpu.VMEM((2, REACH, heads, DH, tile), bf16),
            pltpu.VMEM((2, REACH, heads, DH, tile), bf16),
            pltpu.VMEM((heads, tile, DH), bf16),
            pltpu.VMEM((heads, tile, DH), bf16),
            pltpu.VMEM((heads, tile, DH), bf16),
            dma((heads, 2)),
            dma((heads, 2)),
            dma((2, REACH, heads)),
            dma((2, REACH, heads)),
            dma((heads, SPAN)),
            dma((heads, SPAN)),
            dma((heads, SPAN)),
            dma((heads, SPAN)),
            dma((2, REACH, heads)),
            dma((2, REACH, heads)),
            dma((3,)),
            dma((3,)),
            dma((3, heads)),
        ],
        compiler_params=pltpu.CompilerParams(
            collective_id=0, has_side_effects=True, vmem_limit_bytes=60 * 1024 * 1024
        ),
        cost_estimate=pl.CostEstimate(
            flops=10 * pairs * DH, bytes_accessed=8 * tile * width * 2, transcendentals=pairs
        ),
    )(key_tiles, queries, keys, values, grad_out)


def solution(mesh):
    in_specs = (P("ctx", "head"), P("ctx", "head"), P("ctx", "head"), P("ctx", "head"), P(), P())
    out_specs = (P("ctx", "head", None), P("ctx", "head", None), P("ctx", "head", None))
    return jax.shard_map(shards, mesh=mesh, in_specs=in_specs, out_specs=out_specs, check_vma=False)
```

```python
import functools
import math

import jax
import jax.numpy as jnp
from jax import lax
from jax.experimental import pallas as pl
from jax.experimental.pallas import tpu as pltpu
from jax.sharding import PartitionSpec as P

DH = 128
REACH = 3
SPAN = 2 * REACH + 1
LOW = -1e30
MESH = pl.DeviceIdType.MESH
NT = (((1,), (1,)), ((), ()))

LAG_A = 2
LAG_C = 3
LAG_B = 4


def kernel(
    n_ctx, n_head, heads, tile,
    tiles_hbm, q_hbm, k_hbm, v_hbm, g_hbm,
    dq_hbm, dk_hbm, dv_hbm,
    win, kv, expon, dprob, summit, stat_out, stat_in, res_out, res_in, bias,
    part, hop_out, hop_in, block_q, block_k, block_v,
    load_sem, kv_sem, win_send, win_recv, stat_send, stat_recv, res_send, res_recv,
    hop_send, hop_recv, out_send, out_recv, own_sem, tiles_ref, tiles_sem,
):
    me = lax.axis_index("ctx")
    lane = lax.axis_index("head")
    rows = tile // n_head
    thirds = tile // 128
    scale = DH ** -0.5
    log_scale = scale * math.log2(math.e)

    def at(offset):
        return lax.rem(me + offset + n_ctx, n_ctx)

    tiles_copy = pltpu.make_async_copy(tiles_hbm, tiles_ref, tiles_sem)
    tiles_copy.start()

    barrier = pltpu.get_barrier_semaphore()
    for offset in range(-REACH, REACH + 1):
        if offset != 0:
            pl.semaphore_signal(
                barrier, inc=1, device_id={"ctx": at(offset)}, device_id_type=MESH
            )
    for shift in range(1, n_head):
        pl.semaphore_signal(
            barrier, inc=1, device_id={"head": lax.rem(lane + shift, n_head)},
            device_id_type=MESH,
        )

    def columns(h):
        return pl.ds(pl.multiple_of(h * DH, DH), DH)

    def own_loads(h):
        return [
            pltpu.make_async_copy(q_hbm.at[:, columns(h)], win.at[REACH, h, 0], load_sem.at[h, 0]),
            pltpu.make_async_copy(g_hbm.at[:, columns(h)], win.at[REACH, h, 1], load_sem.at[h, 1]),
        ]

    def kv_loads(h):
        return [
            pltpu.make_async_copy(k_hbm.at[:, columns(h)], kv.at[h, 0], kv_sem.at[h, 0]),
            pltpu.make_async_copy(v_hbm.at[:, columns(h)], kv.at[h, 1], kv_sem.at[h, 1]),
        ]

    @pl.loop(0, heads)
    def _(h):
        for copy in own_loads(h) + kv_loads(h):
            copy.start()

    tiles_copy.wait()
    for p in range(SPAN):
        other = at(p - REACH)
        mine = jnp.zeros((), jnp.bool_)
        theirs = jnp.zeros((), jnp.bool_)
        for j in range(tiles_ref.shape[0]):
            mine = jnp.logical_or(mine, tiles_ref[j, me] == other)
            theirs = jnp.logical_or(theirs, tiles_ref[j, other] == me)
        bias[0, p] = jnp.where(mine, 0.0, LOW)
        bias[1, p] = jnp.where(theirs, 0.0, LOW)

    pl.semaphore_wait(barrier, 2 * REACH + n_head - 1)

    def relay(direction, distance, h):
        step = -1 if direction == 0 else 1
        source = REACH + step * distance
        return pltpu.make_async_remote_copy(
            src_ref=win.at[source, h],
            dst_ref=win.at[source + step, h],
            send_sem=win_send.at[direction, distance, h],
            recv_sem=win_recv.at[direction, distance, h],
            device_id={"ctx": at(-step)},
            device_id_type=MESH,
        )

    def hop(direction, distance, h):
        return pltpu.make_async_remote_copy(
            src_ref=hop_out.at[direction, distance, h],
            dst_ref=hop_in.at[direction, distance, h],
            send_sem=hop_send.at[direction, distance, h],
            recv_sem=hop_recv.at[direction, distance, h],
            device_id={"ctx": at(-1 if direction == 0 else 1)},
            device_id_type=MESH,
        )

    def stat_copy(p, h):
        return pltpu.make_async_remote_copy(
            src_ref=stat_out.at[h, p],
            dst_ref=stat_in.at[h, 2 * REACH - p],
            send_sem=stat_send.at[h, p],
            recv_sem=stat_recv.at[h, 2 * REACH - p],
            device_id={"ctx": at(p - REACH)},
            device_id_type=MESH,
        )

    def res_copy(p, h):
        return pltpu.make_async_remote_copy(
            src_ref=res_out.at[h],
            dst_ref=res_in.at[h, 2 * REACH - p],
            send_sem=res_send.at[h, p],
            recv_sem=res_recv.at[h, 2 * REACH - p],
            device_id={"ctx": at(p - REACH)},
            device_id_type=MESH,
        )

    def spread(block, target, kind, h):
        place = columns(lane * heads + h)
        pltpu.make_async_copy(
            block.at[h, pl.ds(pl.multiple_of(lane * rows, 16), rows), :],
            target.at[0, :, place],
            own_sem.at[kind, h],
        ).start()

        @pl.loop(1, n_head)
        def _(shift):
            peer = lax.rem(lane + shift, n_head)
            pltpu.make_async_remote_copy(
                src_ref=block.at[h, pl.ds(pl.multiple_of(peer * rows, 16), rows), :],
                dst_ref=target.at[0, :, place],
                send_sem=out_send.at[kind],
                recv_sem=out_recv.at[kind],
                device_id={"head": peer},
                device_id_type=MESH,
            ).start()

    def wide(ref, start):
        return jnp.concatenate([ref[start + j : start + j + 1, :] for j in range(thirds)], axis=1)

    def first_pass(first, stride, count, h):
        slot = lax.rem(h, LAG_B - LAG_A)

        @pl.loop(0, count)
        def _(i):
            p = first + stride * i
            scores = lax.dot_general(
                kv[h, 0], win[p, h, 0], NT, preferred_element_type=jnp.float32
            ) * log_scale
            top = jnp.max(scores, axis=0, keepdims=True)
            weights = jnp.exp2(scores - top)
            total = jnp.sum(weights, axis=0, keepdims=True)
            dp = lax.dot_general(kv[h, 1], win[p, h, 1], NT, preferred_element_type=jnp.float32)
            mean = jnp.sum(weights * dp, axis=0, keepdims=True) / total
            expon[slot, p] = weights
            dprob[slot, p] = dp
            summit[slot, p] = top
            level = top + jnp.log2(total)
            for j in range(thirds):
                stat_out[h, p, j : j + 1, :] = level[:, j * 128 : (j + 1) * 128]
                stat_out[h, p, thirds + j : thirds + j + 1, :] = mean[:, j * 128 : (j + 1) * 128]

            @pl.when(p != REACH)
            def _():
                stat_copy(p, h).start()

    def wait_keys(h):
        for copy in kv_loads(h):
            copy.wait()

    def combine(h):
        levels = []
        for p in range(SPAN):
            if p != REACH:
                stat_copy(2 * REACH - p, h).wait_recv()
            source = stat_out if p == REACH else stat_in
            levels.append(source[h, p, 0:thirds, :] + bias[0, p])
        top = functools.reduce(jnp.maximum, levels)
        total = jnp.zeros_like(top)
        delta = jnp.zeros_like(top)
        for p in range(SPAN):
            source = stat_out if p == REACH else stat_in
            weight = jnp.exp2(levels[p] - top)
            total = total + weight
            delta = delta + weight * source[h, p, thirds : 2 * thirds, :]
        level = top + jnp.log2(total)
        delta = delta / total
        res_out[h, 0:thirds, :] = level
        res_out[h, thirds : 2 * thirds, :] = delta
        res_in[h, REACH, 0:thirds, :] = level
        res_in[h, REACH, thirds : 2 * thirds, :] = delta
        for p in range(SPAN):
            if p != REACH:
                res_copy(p, h).start()

    def second_pass(h):
        slot = lax.rem(h, LAG_B - LAG_A)
        keys_turned = kv[h, 0].T

        def body(p, carry):
            dk, dv = carry

            @pl.when(p != REACH)
            def _():
                res_copy(2 * REACH - p, h).wait_recv()

            result = res_in.at[h, p]
            factor = jnp.exp2(summit[slot, p] + bias[1, p] - wide(result, 0))
            delta = wide(result, thirds)
            probs = expon[slot, p] * factor
            dscores = (probs * (dprob[slot, p] - delta)).astype(jnp.bfloat16)
            dv = dv + jnp.dot(
                probs.astype(jnp.bfloat16), win[p, h, 1], preferred_element_type=jnp.float32
            )
            dk = dk + jnp.dot(dscores, win[p, h, 0], preferred_element_type=jnp.float32)
            part[h, p] = (
                jnp.dot(keys_turned, dscores, preferred_element_type=jnp.float32) * scale
            )
            return dk, dv

        start = (jnp.zeros((tile, DH), jnp.float32), jnp.zeros((tile, DH), jnp.float32))
        dk, dv = lax.fori_loop(0, SPAN, body, start)
        for direction, p in ((0, 0), (1, 2 * REACH)):
            hop_out[direction, 0, h] = part[h, p].astype(jnp.bfloat16)
            hop(direction, 0, h).start()
        block_k[h] = (dk * scale).astype(jnp.bfloat16)
        block_v[h] = dv.astype(jnp.bfloat16)
        spread(block_k, dk_hbm, 1, h)
        spread(block_v, dv_hbm, 2, h)

    def pass_on(distance, h):
        for direction, p in ((0, distance), (1, 2 * REACH - distance)):
            hop(direction, distance - 1, h).wait_recv()
            hop_out[direction, distance, h] = (
                part[h, p] + hop_in[direction, distance - 1, h].astype(jnp.float32)
            ).astype(jnp.bfloat16)
            hop(direction, distance, h).start()

    def finish(h):
        total = part[h, REACH]
        for direction in range(2):
            hop(direction, REACH - 1, h).wait_recv()
            total = total + hop_in[direction, REACH - 1, h].astype(jnp.float32)
        block_q[h] = total.T.astype(jnp.bfloat16)
        spread(block_q, dq_hbm, 0, h)

    def send_own(h):
        for copy in own_loads(h):
            copy.wait()
        for direction in range(2):
            relay(direction, 0, h).start()

    send_own(0)

    def during(lag, s, action):
        @pl.when(jnp.logical_and(s >= lag, s < heads + lag))
        def _():
            action(s - lag)

    def forward(distance, h):
        for direction in range(2):
            relay(direction, distance - 1, h).wait_recv()
            if distance < REACH:
                relay(direction, distance, h).start()

    @pl.loop(0, heads + LAG_B + REACH)
    def _(s):
        during(LAG_B + 1, s, functools.partial(pass_on, 1))
        during(2, s, functools.partial(forward, 2))
        during(LAG_B, s, second_pass)
        during(LAG_C, s, combine)
        during(1, s, functools.partial(forward, 1))
        during(LAG_A, s, wait_keys)
        during(LAG_A, s, functools.partial(first_pass, 1, 1, SPAN - 2))
        during(LAG_B + 2, s, functools.partial(pass_on, 2))
        during(LAG_B + 3, s, finish)

        @pl.when(s < heads - 1)
        def _():
            send_own(s + 1)

        during(LAG_A, s, functools.partial(forward, 3))
        during(LAG_A, s, functools.partial(first_pass, 0, SPAN - 1, 2))

    @pl.loop(0, heads)
    def _(h):
        for direction in range(2):
            for distance in range(REACH):
                relay(direction, distance, h).wait_send()
                hop(direction, distance, h).wait_send()
        for p in range(SPAN):
            if p != REACH:
                stat_copy(p, h).wait_send()
                res_copy(p, h).wait_send()
        for kind, (block, target) in enumerate(
            ((block_q, dq_hbm), (block_k, dk_hbm), (block_v, dv_hbm))
        ):
            pltpu.make_async_copy(
                block.at[h, pl.ds(pl.multiple_of(lane * rows, 16), rows), :],
                target.at[0, :, columns(lane * heads + h)],
                own_sem.at[kind, h],
            ).wait()

    for kind, target in enumerate((dq_hbm, dk_hbm, dv_hbm)):
        others = target.at[0, :, pl.ds(0, (n_head - 1) * heads * DH)]
        pltpu.make_async_copy(others, others, out_send.at[kind]).wait()
        pltpu.make_async_copy(others, others, out_recv.at[kind]).wait()


def copy_kernel(a, b, c, a_out, b_out, c_out, sems):
    copies = [
        pltpu.make_async_copy(source, target, sems.at[i])
        for i, (source, target) in enumerate(((a, a_out), (b, b_out), (c, c_out)))
    ]
    for copy in copies:
        copy.start()
    for copy in copies:
        copy.wait()


def shards(queries, keys, values, grad_out, key_tiles, tile_slot):
    tile, width = queries.shape
    heads = width // DH
    n_ctx = lax.axis_size("ctx")
    n_head = lax.axis_size("head")
    rows = tile // n_head
    thirds = tile // 128
    bf16, f32 = jnp.bfloat16, jnp.float32
    dma = pltpu.SemaphoreType.DMA
    out = jax.ShapeDtypeStruct((1, rows, n_head * width), bf16)
    pairs = heads * SPAN * tile * tile
    grads = pl.pallas_call(
        functools.partial(kernel, n_ctx, n_head, heads, tile),
        out_shape=(out, out, out),
        in_specs=[pl.BlockSpec(memory_space=pl.ANY)] * 5,
        out_specs=tuple([pl.BlockSpec(memory_space=pltpu.VMEM)] * 3),
        scratch_shapes=[
            pltpu.VMEM((SPAN, heads, 2, tile, DH), bf16),
            pltpu.VMEM((heads, 2, tile, DH), bf16),
            pltpu.VMEM((LAG_B - LAG_A, SPAN, tile, tile), f32),
            pltpu.VMEM((LAG_B - LAG_A, SPAN, tile, tile), f32),
            pltpu.VMEM((LAG_B - LAG_A, SPAN, 1, tile), f32),
            pltpu.VMEM((heads, SPAN, 2 * thirds, 128), f32),
            pltpu.VMEM((heads, SPAN, 2 * thirds, 128), f32),
            pltpu.VMEM((heads, 2 * thirds, 128), f32),
            pltpu.VMEM((heads, SPAN, 2 * thirds, 128), f32),
            pltpu.SMEM((2, SPAN), f32),
            pltpu.VMEM((heads, SPAN, DH, tile), f32),
            pltpu.VMEM((2, REACH, heads, DH, tile), bf16),
            pltpu.VMEM((2, REACH, heads, DH, tile), bf16),
            pltpu.VMEM((heads, tile, DH), bf16),
            pltpu.VMEM((heads, tile, DH), bf16),
            pltpu.VMEM((heads, tile, DH), bf16),
            dma((heads, 2)),
            dma((heads, 2)),
            dma((2, REACH, heads)),
            dma((2, REACH, heads)),
            dma((heads, SPAN)),
            dma((heads, SPAN)),
            dma((heads, SPAN)),
            dma((heads, SPAN)),
            dma((2, REACH, heads)),
            dma((2, REACH, heads)),
            dma((3,)),
            dma((3,)),
            dma((3, heads)),
            pltpu.SMEM(key_tiles.shape[::-1], jnp.int32),
            dma,
        ],
        compiler_params=pltpu.CompilerParams(
            collective_id=0, has_side_effects=True, vmem_limit_bytes=60 * 1024 * 1024
        ),
        cost_estimate=pl.CostEstimate(
            flops=10 * pairs * DH, bytes_accessed=8 * tile * width * 2, transcendentals=pairs
        ),
    )(key_tiles.T, queries, keys, values, grad_out)
    return pl.pallas_call(
        copy_kernel,
        out_shape=(out, out, out),
        in_specs=[pl.BlockSpec(memory_space=pltpu.VMEM)] * 3,
        out_specs=tuple([pl.BlockSpec(memory_space=pl.ANY)] * 3),
        scratch_shapes=[dma((3,))],
    )(*grads)


def solution(mesh):
    in_specs = (P("ctx", "head"), P("ctx", "head"), P("ctx", "head"), P("ctx", "head"), P(), P())
    out_specs = (P("ctx", "head", None), P("ctx", "head", None), P("ctx", "head", None))
    return jax.shard_map(shards, mesh=mesh, in_specs=in_specs, out_specs=out_specs, check_vma=False)
```

```python
import functools
import math

import jax
import jax.numpy as jnp
from jax import lax
from jax.experimental import pallas as pl
from jax.experimental.pallas import tpu as pltpu
from jax.sharding import PartitionSpec as P

DH = 128
REACH = 3
SPAN = 2 * REACH + 1
LOW = -1e30
MESH = pl.DeviceIdType.MESH
NT = (((1,), (1,)), ((), ()))
RING = 8
RUN = RING // 2
WIDE = RUN + 2 * REACH


def kernel(
    n_ctx, n_head, heads, tile,
    tiles_hbm, q_hbm, k_hbm, v_hbm, g_hbm,
    dq_out, dk_out, dv_out,
    tiles_ref, bias, wide_bias,
    wwin, wkv, wexp, wdp, wtop, wstat, stat_out, stat_in, wres, wdq, edge_out, edge_in, made,
    win, kv, expon, dprob, summit, lone_out, lone_in, res_out, res_in, part, hop_out, hop_in,
    block_q, block_k, block_v,
    tiles_sem, load_sem, in_send, in_recv, side_send, side_recv, wstat_send, wstat_recv,
    wres_send, wres_recv, edge_send, edge_recv, home_send, home_recv,
    win_send, win_recv, stat_send, stat_recv, res_send, res_recv, hop_send, hop_recv,
    out_send, out_recv, own_sem,
):
    me = lax.axis_index("ctx")
    lane = lax.axis_index("head")
    rows = tile // n_head
    thirds = tile // 128
    scale = DH ** -0.5
    log_scale = scale * math.log2(math.e)
    last = heads - 1
    core = lax.rem(lane, 2)
    z = lax.rem(me, RING)
    zl = lax.rem(z, RUN)
    zh = z // RUN
    chip_lane = lane - core
    line = me - z
    first_tile = RUN * (2 * (me // RING) + core)
    stays = zh == core

    def peer(i):
        return (chip_lane + zh, line + RUN * core + i)

    sides = (
        (chip_lane + 1 - core, lax.rem(me - (1 - core) * RING + n_ctx, n_ctx)),
        (chip_lane + 1 - core, lax.rem(me + core * RING, n_ctx)),
    )

    def at(offset):
        return (lane, lax.rem(me + offset + n_ctx, n_ctx))

    def lane_at(shift):
        return (lax.rem(lane + shift, n_head), me)

    tiles_copy = pltpu.make_async_copy(tiles_hbm, tiles_ref, tiles_sem)
    tiles_copy.start()

    barrier = pltpu.get_barrier_semaphore()

    def greet(device):
        pl.semaphore_signal(barrier, inc=1, device_id=device, device_id_type=MESH)

    for i in range(RUN):
        @pl.when(jnp.logical_not(jnp.logical_and(stays, zl == i)))
        def _():
            greet(peer(i))
    for device in sides:
        greet(device)
    for offset in range(-REACH, REACH + 1):
        if offset != 0:
            greet(at(offset))
    for shift in range(1, n_head):
        greet(lane_at(shift))

    def columns(h):
        return pl.ds(pl.multiple_of(h * DH, DH), DH)

    loads = [
        pltpu.make_async_copy(source.at[:, columns(last)], target, load_sem.at[i])
        for i, (source, target) in enumerate((
            (q_hbm, win.at[REACH, 0]), (g_hbm, win.at[REACH, 1]),
            (k_hbm, kv.at[0]), (v_hbm, kv.at[1]),
        ))
    ]
    for copy in loads:
        copy.start()

    def landing(a, j):
        return wwin.at[REACH + a, j] if j < 2 else wkv.at[a, j - 2]

    sources = (q_hbm, g_hbm, k_hbm, v_hbm)

    def in_copy(r, j):
        i = lax.rem(zl + r, RUN)
        return pltpu.make_async_remote_copy(
            src_ref=sources[j].at[:, columns(i)],
            dst_ref=landing(zl, j),
            send_sem=in_send.at[r, j],
            recv_sem=in_recv.at[zl, j],
            device_id=peer(i),
            device_id_type=MESH,
        )

    def in_wait(a, j):
        pltpu.make_async_remote_copy(
            src_ref=sources[j].at[:, columns(a)],
            dst_ref=landing(a, j),
            send_sem=in_send.at[0, j],
            recv_sem=in_recv.at[a, j],
            device_id=peer(a),
            device_id_type=MESH,
        ).wait_recv()

    tiles_copy.wait()

    def listed(query_tile, key_tile):
        found = jnp.zeros((), jnp.bool_)
        for j in range(tiles_ref.shape[0]):
            found = jnp.logical_or(found, tiles_ref[j, query_tile] == key_tile)
        return jnp.where(found, 0.0, LOW)

    pl.semaphore_wait(
        barrier, 2 + 2 * REACH + n_head - 1 + RUN - jnp.where(stays, 1, 0).astype(jnp.int32)
    )

    for r, j in [(r, j) for pair in ((0, 1), (2, 3)) for r in range(RUN) for j in pair]:
        if True:
            if r > 0:
                in_copy(r, j).start()
            else:
                @pl.when(stays)
                def _():
                    pltpu.make_async_copy(
                        sources[j].at[:, columns(zl)], landing(zl, j), in_recv.at[zl, j]
                    ).start()

                @pl.when(jnp.logical_not(stays))
                def _():
                    in_copy(0, j).start()

    def relay(direction, distance):
        step = -1 if direction == 0 else 1
        source = REACH + step * distance
        return pltpu.make_async_remote_copy(
            src_ref=win.at[source],
            dst_ref=win.at[source + step],
            send_sem=win_send.at[direction, distance],
            recv_sem=win_recv.at[direction, distance],
            device_id=at(-step),
            device_id_type=MESH,
        )

    def forward(distance):
        for direction in range(2):
            relay(direction, distance - 1).wait_recv()
            if distance < REACH:
                relay(direction, distance).start()

    def hop(direction, distance):
        return pltpu.make_async_remote_copy(
            src_ref=hop_out.at[direction, distance],
            dst_ref=hop_in.at[direction, distance],
            send_sem=hop_send.at[direction, distance],
            recv_sem=hop_recv.at[direction, distance],
            device_id=at(-1 if direction == 0 else 1),
            device_id_type=MESH,
        )

    def stat_copy(p):
        return pltpu.make_async_remote_copy(
            src_ref=lone_out.at[p],
            dst_ref=lone_in.at[2 * REACH - p],
            send_sem=stat_send.at[p],
            recv_sem=stat_recv.at[2 * REACH - p],
            device_id=at(p - REACH),
            device_id_type=MESH,
        )

    def res_copy(p):
        return pltpu.make_async_remote_copy(
            src_ref=res_out,
            dst_ref=res_in.at[2 * REACH - p],
            send_sem=res_send.at[p],
            recv_sem=res_recv.at[2 * REACH - p],
            device_id=at(p - REACH),
            device_id_type=MESH,
        )

    def side_copy(side, a):
        shift = RUN if side == 0 else -RUN
        slot = a if side == 0 else a - 1
        return pltpu.make_async_remote_copy(
            src_ref=wwin.at[REACH + a],
            dst_ref=wwin.at[REACH + a + shift],
            send_sem=side_send.at[side, slot],
            recv_sem=side_recv.at[side, slot],
            device_id=sides[side],
            device_id_type=MESH,
        )

    def wstat_copy(side):
        return pltpu.make_async_remote_copy(
            src_ref=stat_out.at[side],
            dst_ref=stat_in.at[1 - side],
            send_sem=wstat_send.at[side],
            recv_sem=wstat_recv.at[1 - side],
            device_id=sides[side],
            device_id_type=MESH,
        )

    def wres_copy(side):
        return pltpu.make_async_remote_copy(
            src_ref=wres.at[pl.ds(REACH + side, REACH)],
            dst_ref=wres.at[pl.ds(REACH + RUN if side == 0 else 0, REACH)],
            send_sem=wres_send.at[side],
            recv_sem=wres_recv.at[1 - side],
            device_id=sides[side],
            device_id_type=MESH,
        )

    def edge_copy(side):
        return pltpu.make_async_remote_copy(
            src_ref=edge_out.at[side],
            dst_ref=edge_in.at[1 - side],
            send_sem=edge_send.at[side],
            recv_sem=edge_recv.at[1 - side],
            device_id=sides[side],
            device_id_type=MESH,
        )

    blocks = (block_q, block_k, block_v)
    targets = (dq_out, dk_out, dv_out)

    def home_copy(kind, i):
        return pltpu.make_async_remote_copy(
            src_ref=made.at[kind, i],
            dst_ref=blocks[kind].at[zl],
            send_sem=home_send.at[kind, i],
            recv_sem=home_recv.at[kind, zl],
            device_id=peer(i),
            device_id_type=MESH,
        )

    def home_local(kind, i):
        return pltpu.make_async_copy(
            made.at[kind, i], blocks[kind].at[zl], home_recv.at[kind, zl]
        )

    def go_home(kind, i):
        mine = jnp.logical_and(stays, zl == i)

        @pl.when(mine)
        def _():
            home_local(kind, i).start()

        @pl.when(jnp.logical_not(mine))
        def _():
            home_copy(kind, i).start()

    def own_part(kind, h):
        return pltpu.make_async_copy(
            blocks[kind].at[h, pl.ds(pl.multiple_of(lane * rows, 16), rows), :],
            targets[kind].at[0, :, columns(lane * heads + h)],
            own_sem.at[kind, h],
        )

    def spread(kind, h):
        own_part(kind, h).start()

        @pl.loop(1, n_head)
        def _(shift):
            device = lane_at(shift)
            pltpu.make_async_remote_copy(
                src_ref=blocks[kind].at[h, pl.ds(pl.multiple_of(device[0] * rows, 16), rows), :],
                dst_ref=targets[kind].at[0, :, columns(lane * heads + h)],
                send_sem=out_send.at[kind],
                recv_sem=out_recv.at[kind],
                device_id=device,
                device_id_type=MESH,
            ).start()

    def arrived(kind, h):
        pltpu.make_async_remote_copy(
            src_ref=made.at[kind, 0],
            dst_ref=blocks[kind].at[h],
            send_sem=home_send.at[kind, 0],
            recv_sem=home_recv.at[kind, h],
            device_id=peer(h),
            device_id_type=MESH,
        ).wait_recv()

    def wide(ref, start):
        return jnp.concatenate([ref[start + j : start + j + 1, :] for j in range(thirds)], axis=1)

    def score(key, value, query, grad, weights_ref, dp_ref, top_ref, stat_ref):
        scores = lax.dot_general(
            key[...], query[...], NT, preferred_element_type=jnp.float32
        ) * log_scale
        top = jnp.max(scores, axis=0, keepdims=True)
        weights = jnp.exp2(scores - top)
        total = jnp.sum(weights, axis=0, keepdims=True)
        dp = lax.dot_general(value[...], grad[...], NT, preferred_element_type=jnp.float32)
        mean = jnp.sum(weights * dp, axis=0, keepdims=True) / total
        weights_ref[...] = weights
        dp_ref[...] = dp
        top_ref[...] = top
        level = top + jnp.log2(total)
        for j in range(thirds):
            stat_ref[j : j + 1, :] = level[:, j * 128 : (j + 1) * 128]
            stat_ref[thirds + j : thirds + j + 1, :] = mean[:, j * 128 : (j + 1) * 128]

    def merge(parts):
        top = functools.reduce(jnp.maximum, [level for level, _ in parts])
        total = jnp.zeros_like(top)
        mean = jnp.zeros_like(top)
        for level, value in parts:
            weight = jnp.exp2(level - top)
            total = total + weight
            mean = mean + weight * value
        return top + jnp.log2(total), mean / total

    def put(ref, pair):
        ref[0:thirds, :] = pair[0]
        ref[thirds : 2 * thirds, :] = pair[1]

    def gradients(weights_ref, dp_ref, top_ref, offset, result, query, grad, turned):
        factor = jnp.exp2(top_ref[...] + offset - wide(result, 0))
        probs = weights_ref[...] * factor
        dscores = (probs * (dp_ref[...] - wide(result, thirds))).astype(jnp.bfloat16)
        dv = jnp.dot(probs.astype(jnp.bfloat16), grad[...], preferred_element_type=jnp.float32)
        dk = jnp.dot(dscores, query[...], preferred_element_type=jnp.float32)
        return dk, dv, jnp.dot(turned, dscores, preferred_element_type=jnp.float32)

    def wide_score(i, p):
        o = p - i
        score(
            wkv.at[i, 0], wkv.at[i, 1], wwin.at[p, 0], wwin.at[p, 1],
            wexp.at[i, o], wdp.at[i, o], wtop.at[i, o], wstat.at[i, o],
        )

    def local_parts(p):
        return [
            (
                wstat[i, p - i, 0:thirds, :] + wide_bias[i, p - i],
                wstat[i, p - i, thirds : 2 * thirds, :],
            )
            for i in range(RUN)
            if 0 <= p - i < SPAN
        ]

    def wide_gradients(i):
        turned = wkv[i, 0].T

        def body(o, carry):
            p = i + o
            dk, dv, dq = gradients(
                wexp.at[i, o], wdp.at[i, o], wtop.at[i, o], wide_bias[i, o], wres.at[p],
                wwin.at[p, 0], wwin.at[p, 1], turned,
            )
            wdq[p] = wdq[p] + dq
            return carry[0] + dk, carry[1] + dv

        start = (jnp.zeros((tile, DH), jnp.float32), jnp.zeros((tile, DH), jnp.float32))
        dk, dv = lax.fori_loop(0, SPAN, body, start)
        made[1, i] = (dk * scale).astype(jnp.bfloat16)
        made[2, i] = dv.astype(jnp.bfloat16)
        go_home(1, i)
        go_home(2, i)

    def send_edge(side):
        for i in range(REACH):
            edge_out[side, i] = wdq[i if side == 0 else REACH + RUN + i].astype(jnp.bfloat16)
        edge_copy(side).start()

    def lone_score(first, stride, count):
        @pl.loop(0, count)
        def _(i):
            p = first + stride * i
            score(
                kv.at[0], kv.at[1], win.at[p, 0], win.at[p, 1],
                expon.at[p], dprob.at[p], summit.at[p], lone_out.at[p],
            )

            @pl.when(p != REACH)
            def _():
                stat_copy(p).start()

    def lone_combine():
        parts = []
        for p in range(SPAN):
            if p != REACH:
                stat_copy(2 * REACH - p).wait_recv()
            source = lone_out if p == REACH else lone_in
            parts.append(
                (source[p, 0:thirds, :] + bias[0, p], source[p, thirds : 2 * thirds, :])
            )
        pair = merge(parts)
        put(res_out, pair)
        put(res_in.at[REACH], pair)
        for p in range(SPAN):
            if p != REACH:
                res_copy(p).start()

    def lone_gradients():
        turned = kv[0].T

        def body(p, carry):
            @pl.when(p != REACH)
            def _():
                res_copy(2 * REACH - p).wait_recv()

            dk, dv, dq = gradients(
                expon.at[p], dprob.at[p], summit.at[p], bias[1, p], res_in.at[p],
                win.at[p, 0], win.at[p, 1], turned,
            )
            part[p] = dq
            return carry[0] + dk, carry[1] + dv

        start = (jnp.zeros((tile, DH), jnp.float32), jnp.zeros((tile, DH), jnp.float32))
        dk, dv = lax.fori_loop(0, SPAN, body, start)
        for direction, p in ((0, 0), (1, 2 * REACH)):
            hop_out[direction, 0] = part[p].astype(jnp.bfloat16)
            hop(direction, 0).start()
        block_k[last] = (dk * scale).astype(jnp.bfloat16)
        block_v[last] = dv.astype(jnp.bfloat16)
        spread(1, last)
        spread(2, last)

    def pass_on(distance):
        for direction, p in ((0, distance), (1, 2 * REACH - distance)):
            hop(direction, distance - 1).wait_recv()
            hop_out[direction, distance] = (
                part[p] + hop_in[direction, distance - 1].astype(jnp.float32)
            ).astype(jnp.bfloat16)
            hop(direction, distance).start()

    def lone_finish():
        total = part[REACH]
        for direction in range(2):
            hop(direction, REACH - 1).wait_recv()
            total = total + hop_in[direction, REACH - 1].astype(jnp.float32)
        block_q[last] = (total * scale).T.astype(jnp.bfloat16)
        spread(0, last)

    for copy in loads:
        copy.wait()
    for direction in range(2):
        relay(direction, 0).start()

    wdq[...] = jnp.zeros_like(wdq)
    for p in range(SPAN):
        other = lax.rem(me + p - REACH + n_ctx, n_ctx)
        bias[0, p] = listed(me, other)
        bias[1, p] = listed(other, me)
    for i in range(RUN):
        for o in range(SPAN):
            query_tile = lax.rem(first_tile + i + o - REACH + n_ctx, n_ctx)
            wide_bias[i, o] = listed(query_tile, first_tile + i)

    def received(r):
        return lax.rem(zl - r + RUN, RUN)

    for r in range(RUN):
        newest = received(r)
        for j in range(2):
            in_wait(newest, j)

        @pl.when(newest < REACH)
        def _():
            side_copy(0, newest).start()

        @pl.when(newest >= RUN - REACH)
        def _():
            side_copy(1, newest).start()

    for k in range(REACH):
        side_copy(0, k).wait_recv()
        side_copy(1, k + 1).wait_recv()

    @pl.loop(0, RUN)
    def _(r):
        newest = received(r)
        for j in range(2, 4):
            in_wait(newest, j)

        @pl.loop(0, SPAN)
        def _(o):
            wide_score(newest, newest + o)

    for side in range(2):
        for p in range(REACH):
            put(stat_out.at[side, p], merge(local_parts(p + (REACH + RUN) * side)))
        wstat_copy(side).start()

    lone_score(REACH, 1, 1)
    forward(1)
    lone_score(REACH - 1, 2, 2)

    for side in range(2):
        wstat_copy(side).wait_recv()
    for a in range(RUN):
        parts = local_parts(REACH + a)
        if a < REACH:
            parts.append((stat_in[0, a, 0:thirds, :], stat_in[0, a, thirds : 2 * thirds, :]))
        if a >= RUN - REACH:
            b = a - (RUN - REACH)
            parts.append((stat_in[1, b, 0:thirds, :], stat_in[1, b, thirds : 2 * thirds, :]))
        put(wres.at[REACH + a], merge(parts))
    for side in range(2):
        wres_copy(side).start()

    forward(2)
    lone_score(REACH - 2, 4, 2)

    for side in range(2):
        wres_copy(side).wait_recv()

    def home_round(kind, r):
        h = received(r)
        arrived(kind, h)
        spread(kind, h)

    wide_gradients(zl)
    forward(3)
    lone_score(0, SPAN - 1, 2)
    wide_gradients(lax.rem(zl + 1, RUN))
    lone_combine()
    home_round(1, 0)
    home_round(2, 0)
    wide_gradients(lax.rem(zl + 2, RUN))
    home_round(1, 1)
    home_round(2, 1)
    wide_gradients(lax.rem(zl + 3, RUN))
    send_edge(0)
    send_edge(1)
    lone_gradients()
    home_round(1, 2)
    home_round(2, 2)
    pass_on(1)

    for side in range(2):
        edge_copy(side).wait_recv()
    for a in range(RUN):
        total = wdq[REACH + a]
        if a < REACH:
            total = total + edge_in[0, a].astype(jnp.float32)
        if a >= RUN - REACH:
            total = total + edge_in[1, a - (RUN - REACH)].astype(jnp.float32)
        made[0, a] = (total * scale).T.astype(jnp.bfloat16)
    for r in range(RUN):
        go_home(0, lax.rem(zl + r, RUN))

    pass_on(2)
    home_round(1, 3)
    home_round(2, 3)
    for r in range(RUN):
        home_round(0, r)
    lone_finish()

    for r in range(RUN):
        for j in range(4):
            if r > 0:
                in_copy(r, j).wait_send()
            else:
                @pl.when(jnp.logical_not(stays))
                def _():
                    in_copy(0, j).wait_send()
    for side in range(2):
        for a in range(REACH):
            side_copy(side, a + side).wait_send()
        wstat_copy(side).wait_send()
        wres_copy(side).wait_send()
        edge_copy(side).wait_send()
    for kind in range(3):
        for i in range(RUN):
            @pl.when(jnp.logical_not(jnp.logical_and(stays, zl == i)))
            def _():
                home_copy(kind, i).wait_send()
    for direction in range(2):
        for distance in range(REACH):
            relay(direction, distance).wait_send()
            hop(direction, distance).wait_send()
    for p in range(SPAN):
        if p != REACH:
            stat_copy(p).wait_send()
            res_copy(p).wait_send()
    for kind, target in enumerate(targets):
        for h in range(heads):
            own_part(kind, h).wait()
        others = target.at[0, :, pl.ds(0, (n_head - 1) * heads * DH)]
        pltpu.make_async_copy(others, others, out_send.at[kind]).wait()
        pltpu.make_async_copy(others, others, out_recv.at[kind]).wait()


def copy_kernel(a, b, c, a_out, b_out, c_out, sems):
    copies = [
        pltpu.make_async_copy(source, target, sems.at[i])
        for i, (source, target) in enumerate(((a, a_out), (b, b_out), (c, c_out)))
    ]
    for copy in copies:
        copy.start()
    for copy in copies:
        copy.wait()


def shards(queries, keys, values, grad_out, key_tiles, tile_slot):
    tile, width = queries.shape
    heads = width // DH
    n_ctx = lax.axis_size("ctx")
    n_head = lax.axis_size("head")
    rows = tile // n_head
    lines = 2 * (tile // 128)
    bf16, f32 = jnp.bfloat16, jnp.float32
    dma, vmem, smem = pltpu.SemaphoreType.DMA, pltpu.VMEM, pltpu.SMEM
    out = jax.ShapeDtypeStruct((1, rows, n_head * width), bf16)
    pairs = heads * SPAN * tile * tile
    grads = pl.pallas_call(
        functools.partial(kernel, n_ctx, n_head, heads, tile),
        out_shape=(out, out, out),
        in_specs=[pl.BlockSpec(memory_space=pl.ANY)] * 5,
        out_specs=tuple([pl.BlockSpec(memory_space=pltpu.VMEM)] * 3),
        scratch_shapes=[
            smem(key_tiles.shape[::-1], jnp.int32),
            smem((2, SPAN), f32),
            smem((RUN, SPAN), f32),
            vmem((WIDE, 2, tile, DH), bf16),
            vmem((RUN, 2, tile, DH), bf16),
            vmem((RUN, SPAN, tile, tile), f32),
            vmem((RUN, SPAN, tile, tile), f32),
            vmem((RUN, SPAN, 1, tile), f32),
            vmem((RUN, SPAN, lines, 128), f32),
            vmem((2, REACH, lines, 128), f32),
            vmem((2, REACH, lines, 128), f32),
            vmem((WIDE, lines, 128), f32),
            vmem((WIDE, DH, tile), f32),
            vmem((2, REACH, DH, tile), bf16),
            vmem((2, REACH, DH, tile), bf16),
            vmem((3, RUN, tile, DH), bf16),
            vmem((SPAN, 2, tile, DH), bf16),
            vmem((2, tile, DH), bf16),
            vmem((SPAN, tile, tile), f32),
            vmem((SPAN, tile, tile), f32),
            vmem((SPAN, 1, tile), f32),
            vmem((SPAN, lines, 128), f32),
            vmem((SPAN, lines, 128), f32),
            vmem((lines, 128), f32),
            vmem((SPAN, lines, 128), f32),
            vmem((SPAN, DH, tile), f32),
            vmem((2, REACH, DH, tile), bf16),
            vmem((2, REACH, DH, tile), bf16),
            vmem((heads, tile, DH), bf16),
            vmem((heads, tile, DH), bf16),
            vmem((heads, tile, DH), bf16),
            dma,
            dma((4,)),
            dma((RUN, 4)),
            dma((RUN, 4)),
            dma((2, REACH)),
            dma((2, REACH)),
            dma((2,)),
            dma((2,)),
            dma((2,)),
            dma((2,)),
            dma((2,)),
            dma((2,)),
            dma((3, RUN)),
            dma((3, RUN)),
            dma((2, REACH)),
            dma((2, REACH)),
            dma((SPAN,)),
            dma((SPAN,)),
            dma((SPAN,)),
            dma((SPAN,)),
            dma((2, REACH)),
            dma((2, REACH)),
            dma((3,)),
            dma((3,)),
            dma((3, heads)),
        ],
        compiler_params=pltpu.CompilerParams(
            collective_id=0, has_side_effects=True, vmem_limit_bytes=62 * 1024 * 1024
        ),
        cost_estimate=pl.CostEstimate(
            flops=10 * pairs * DH, bytes_accessed=8 * tile * width * 2, transcendentals=pairs
        ),
    )(key_tiles.T, queries, keys, values, grad_out)
    return pl.pallas_call(
        copy_kernel,
        out_shape=(out, out, out),
        in_specs=[pl.BlockSpec(memory_space=pltpu.VMEM)] * 3,
        out_specs=tuple([pl.BlockSpec(memory_space=pl.ANY)] * 3),
        scratch_shapes=[dma((3,))],
    )(*grads)


def solution(mesh):
    in_specs = (P("ctx", "head"), P("ctx", "head"), P("ctx", "head"), P("ctx", "head"), P(), P())
    out_specs = (P("ctx", "head", None), P("ctx", "head", None), P("ctx", "head", None))
    return jax.shard_map(shards, mesh=mesh, in_specs=in_specs, out_specs=out_specs, check_vma=False)
```

```python
import functools
import math

import jax
import jax.numpy as jnp
from jax import lax
from jax.experimental import pallas as pl
from jax.experimental.pallas import tpu as pltpu
from jax.sharding import PartitionSpec as P

DH = 128
REACH = 3
SPAN = 2 * REACH + 1
LOW = -1e30
MESH = pl.DeviceIdType.MESH
NT = (((1,), (1,)), ((), ()))
QUERY_SIDE, KEY_SIDE = (0, 1), (2, 3)
RING = 8
RUN = RING // 2
WIDE = RUN + 2 * REACH


def kernel(
    n_ctx, n_head, heads, tile,
    tiles_hbm, q_hbm, k_hbm, v_hbm, g_hbm,
    dq_out, dk_out, dv_out,
    tiles_ref, bias, wide_bias,
    wwin, wkv, wexp, wdp, wtop, wstat, part_stat, edge_stat, own_stat, far_stat, wres, wdq, edge_out, edge_in, made,
    win, kv, expon, dprob, summit, lone_out, lone_in, res_out, res_in, part, hop_out, hop_in,
    block_q, block_k, block_v,
    tiles_sem, load_sem, in_send, in_recv, side_send, side_recv, wstat_send, wstat_recv,
    edge_send, edge_recv, home_send, home_recv,
    win_send, win_recv, stat_send, stat_recv, res_send, res_recv, hop_send, hop_recv,
    out_send, out_recv, own_sem,
):
    me = lax.axis_index("ctx")
    lane = lax.axis_index("head")
    rows = tile // n_head
    thirds = tile // 128
    scale = DH ** -0.5
    log_scale = scale * math.log2(math.e)
    last = heads - 1
    core = lax.rem(lane, 2)
    z = lax.rem(me, RING)
    zl = lax.rem(z, RUN)
    zh = z // RUN
    chip_lane = lane - core
    line = me - z
    first_tile = RUN * (2 * (me // RING) + core)
    stays = zh == core

    def peer(i):
        return (chip_lane + zh, line + RUN * core + i)

    sides = (
        (chip_lane + 1 - core, lax.rem(me - (1 - core) * RING + n_ctx, n_ctx)),
        (chip_lane + 1 - core, lax.rem(me + core * RING, n_ctx)),
    )

    far_sides = (
        (lane, lax.rem(me - RING + n_ctx, n_ctx)),
        (lane, lax.rem(me + RING, n_ctx)),
    )

    def at(offset):
        return (lane, lax.rem(me + offset + n_ctx, n_ctx))

    def lane_at(shift):
        return (lax.rem(lane + shift, n_head), me)

    tiles_copy = pltpu.make_async_copy(tiles_hbm, tiles_ref, tiles_sem)
    tiles_copy.start()

    barrier = pltpu.get_barrier_semaphore()

    def greet(device):
        pl.semaphore_signal(barrier, inc=1, device_id=device, device_id_type=MESH)

    for i in range(RUN):
        @pl.when(jnp.logical_not(jnp.logical_and(stays, zl == i)))
        def _():
            greet(peer(i))
    for device in sides + far_sides:
        greet(device)
    for offset in range(-REACH, REACH + 1):
        if offset != 0:
            greet(at(offset))
    for shift in range(1, n_head):
        greet(lane_at(shift))

    def columns(h):
        return pl.ds(pl.multiple_of(h * DH, DH), DH)

    loads = [
        pltpu.make_async_copy(source.at[:, columns(last)], target, load_sem.at[i])
        for i, (source, target) in enumerate((
            (q_hbm, win.at[REACH, 0]), (g_hbm, win.at[REACH, 1]),
            (k_hbm, kv.at[0]), (v_hbm, kv.at[1]),
        ))
    ]
    for copy in loads:
        copy.start()

    def landing(a, j):
        return wwin.at[REACH + a, j] if j < 2 else wkv.at[a, j - 2]

    sources = (q_hbm, g_hbm, k_hbm, v_hbm)

    def in_copy(r, j):
        i = lax.rem(zl + r, RUN)
        return pltpu.make_async_remote_copy(
            src_ref=sources[j].at[:, columns(i)],
            dst_ref=landing(zl, j),
            send_sem=in_send.at[r, j],
            recv_sem=in_recv.at[zl, j],
            device_id=peer(i),
            device_id_type=MESH,
        )

    def in_wait(a, j):
        pltpu.make_async_remote_copy(
            src_ref=sources[j].at[:, columns(a)],
            dst_ref=landing(a, j),
            send_sem=in_send.at[0, j],
            recv_sem=in_recv.at[a, j],
            device_id=peer(a),
            device_id_type=MESH,
        ).wait_recv()

    tiles_copy.wait()

    def listed(query_tile, key_tile):
        found = jnp.zeros((), jnp.bool_)
        for j in range(tiles_ref.shape[0]):
            found = jnp.logical_or(found, tiles_ref[j, query_tile] == key_tile)
        return jnp.where(found, 0.0, LOW)

    pl.semaphore_wait(
        barrier, 4 + 2 * REACH + n_head - 1 + RUN - jnp.where(stays, 1, 0).astype(jnp.int32)
    )

    def send_in(r, pair):
        for j in pair:
            if r > 0:
                in_copy(r, j).start()
            else:
                @pl.when(stays)
                def _():
                    pltpu.make_async_copy(
                        sources[j].at[:, columns(zl)], landing(zl, j), in_recv.at[zl, j]
                    ).start()

                @pl.when(jnp.logical_not(stays))
                def _():
                    in_copy(0, j).start()

    def relay(direction, distance):
        step = -1 if direction == 0 else 1
        source = REACH + step * distance
        return pltpu.make_async_remote_copy(
            src_ref=win.at[source],
            dst_ref=win.at[source + step],
            send_sem=win_send.at[direction, distance],
            recv_sem=win_recv.at[direction, distance],
            device_id=at(-step),
            device_id_type=MESH,
        )

    def forward(distance):
        for direction in range(2):
            relay(direction, distance - 1).wait_recv()
            if distance < REACH:
                relay(direction, distance).start()

    def hop(direction, distance):
        return pltpu.make_async_remote_copy(
            src_ref=hop_out.at[direction, distance],
            dst_ref=hop_in.at[direction, distance],
            send_sem=hop_send.at[direction, distance],
            recv_sem=hop_recv.at[direction, distance],
            device_id=at(-1 if direction == 0 else 1),
            device_id_type=MESH,
        )

    def stat_copy(p):
        return pltpu.make_async_remote_copy(
            src_ref=lone_out.at[p],
            dst_ref=lone_in.at[2 * REACH - p],
            send_sem=stat_send.at[p],
            recv_sem=stat_recv.at[2 * REACH - p],
            device_id=at(p - REACH),
            device_id_type=MESH,
        )

    def res_copy(p):
        return pltpu.make_async_remote_copy(
            src_ref=res_out,
            dst_ref=res_in.at[2 * REACH - p],
            send_sem=res_send.at[p],
            recv_sem=res_recv.at[2 * REACH - p],
            device_id=at(p - REACH),
            device_id_type=MESH,
        )

    def side_copy(side, a):
        shift = RUN if side == 0 else -RUN
        slot = a if side == 0 else a - 1
        return pltpu.make_async_remote_copy(
            src_ref=wwin.at[REACH + a],
            dst_ref=wwin.at[REACH + a + shift],
            send_sem=side_send.at[side, slot],
            recv_sem=side_recv.at[side, slot],
            device_id=sides[side],
            device_id_type=MESH,
        )

    def wstat_copy(side, what):
        first, count, inbox, device = (
            (WIDE - REACH if side else 0, REACH, edge_stat, sides[side]),
            (REACH, RUN, own_stat, sides[side]),
            (WIDE - REACH if side else 0, REACH, far_stat, far_sides[side]),
        )[what]
        return pltpu.make_async_remote_copy(
            src_ref=part_stat.at[pl.ds(first, count)],
            dst_ref=inbox.at[1 - side],
            send_sem=wstat_send.at[side, what],
            recv_sem=wstat_recv.at[1 - side, what],
            device_id=device,
            device_id_type=MESH,
        )

    def edge_copy(side):
        return pltpu.make_async_remote_copy(
            src_ref=edge_out.at[side],
            dst_ref=edge_in.at[1 - side],
            send_sem=edge_send.at[side],
            recv_sem=edge_recv.at[1 - side],
            device_id=sides[side],
            device_id_type=MESH,
        )

    blocks = (block_q, block_k, block_v)
    targets = (dq_out, dk_out, dv_out)

    def home_copy(kind, i):
        return pltpu.make_async_remote_copy(
            src_ref=made.at[kind, i],
            dst_ref=blocks[kind].at[zl],
            send_sem=home_send.at[kind, i],
            recv_sem=home_recv.at[kind, zl],
            device_id=peer(i),
            device_id_type=MESH,
        )

    def home_local(kind, i):
        return pltpu.make_async_copy(
            made.at[kind, i], blocks[kind].at[zl], home_recv.at[kind, zl]
        )

    def go_home(kind, i):
        mine = jnp.logical_and(stays, zl == i)

        @pl.when(mine)
        def _():
            home_local(kind, i).start()

        @pl.when(jnp.logical_not(mine))
        def _():
            home_copy(kind, i).start()

    def own_part(kind, h):
        return pltpu.make_async_copy(
            blocks[kind].at[h, pl.ds(pl.multiple_of(lane * rows, 16), rows), :],
            targets[kind].at[0, :, columns(lane * heads + h)],
            own_sem.at[kind, h],
        )

    def spread(kind, h):
        own_part(kind, h).start()

        @pl.loop(1, n_head)
        def _(shift):
            device = lane_at(shift)
            pltpu.make_async_remote_copy(
                src_ref=blocks[kind].at[h, pl.ds(pl.multiple_of(device[0] * rows, 16), rows), :],
                dst_ref=targets[kind].at[0, :, columns(lane * heads + h)],
                send_sem=out_send.at[kind],
                recv_sem=out_recv.at[kind],
                device_id=device,
                device_id_type=MESH,
            ).start()

    def arrived(kind, h):
        pltpu.make_async_remote_copy(
            src_ref=made.at[kind, 0],
            dst_ref=blocks[kind].at[h],
            send_sem=home_send.at[kind, 0],
            recv_sem=home_recv.at[kind, h],
            device_id=peer(h),
            device_id_type=MESH,
        ).wait_recv()

    def wide(ref, start):
        return jnp.concatenate([ref[start + j : start + j + 1, :] for j in range(thirds)], axis=1)

    def score(key, value, query, grad, weights_ref, dp_ref, top_ref, stat_ref):
        scores = lax.dot_general(
            key[...], query[...], NT, preferred_element_type=jnp.float32
        ) * log_scale
        top = jnp.max(scores, axis=0, keepdims=True)
        weights = jnp.exp2(scores - top)
        total = jnp.sum(weights, axis=0, keepdims=True)
        dp = lax.dot_general(value[...], grad[...], NT, preferred_element_type=jnp.float32)
        mean = jnp.sum(weights * dp, axis=0, keepdims=True) / total
        weights_ref[...] = weights
        dp_ref[...] = dp
        top_ref[...] = top
        level = top + jnp.log2(total)
        for j in range(thirds):
            stat_ref[j : j + 1, :] = level[:, j * 128 : (j + 1) * 128]
            stat_ref[thirds + j : thirds + j + 1, :] = mean[:, j * 128 : (j + 1) * 128]

    def merge(parts):
        top = functools.reduce(jnp.maximum, [level for level, _ in parts])
        total = jnp.zeros_like(top)
        mean = jnp.zeros_like(top)
        for level, value in parts:
            weight = jnp.exp2(level - top)
            total = total + weight
            mean = mean + weight * value
        return top + jnp.log2(total), mean / total

    def put(ref, pair):
        ref[0:thirds, :] = pair[0]
        ref[thirds : 2 * thirds, :] = pair[1]

    def gradients(weights_ref, dp_ref, top_ref, offset, result, query, grad, turned):
        factor = jnp.exp2(top_ref[...] + offset - wide(result, 0))
        probs = weights_ref[...] * factor
        dscores = (probs * (dp_ref[...] - wide(result, thirds))).astype(jnp.bfloat16)
        dv = jnp.dot(probs.astype(jnp.bfloat16), grad[...], preferred_element_type=jnp.float32)
        dk = jnp.dot(dscores, query[...], preferred_element_type=jnp.float32)
        return dk, dv, jnp.dot(turned, dscores, preferred_element_type=jnp.float32)

    def wide_score(i, p):
        o = p - i
        score(
            wkv.at[i, 0], wkv.at[i, 1], wwin.at[p, 0], wwin.at[p, 1],
            wexp.at[i, o], wdp.at[i, o], wtop.at[i, o], wstat.at[i, o],
        )

    def local_parts(p):
        return [
            (
                wstat[i, p - i, 0:thirds, :] + wide_bias[i, p - i],
                wstat[i, p - i, thirds : 2 * thirds, :],
            )
            for i in range(RUN)
            if 0 <= p - i < SPAN
        ]

    def wide_gradients(i):
        turned = wkv[i, 0].T

        def body(o, carry):
            p = i + o
            dk, dv, dq = gradients(
                wexp.at[i, o], wdp.at[i, o], wtop.at[i, o], wide_bias[i, o], wres.at[p],
                wwin.at[p, 0], wwin.at[p, 1], turned,
            )
            wdq[p] = wdq[p] + dq
            return carry[0] + dk, carry[1] + dv

        start = (jnp.zeros((tile, DH), jnp.float32), jnp.zeros((tile, DH), jnp.float32))
        dk, dv = lax.fori_loop(0, SPAN, body, start, unroll=SPAN)
        made[1, i] = (dk * scale).astype(jnp.bfloat16)
        made[2, i] = dv.astype(jnp.bfloat16)
        go_home(1, i)
        go_home(2, i)

    def send_edge(side):
        for i in range(REACH):
            edge_out[side, i] = wdq[i if side == 0 else REACH + RUN + i].astype(jnp.bfloat16)
        edge_copy(side).start()

    def lone_score(first, stride, count):
        @pl.loop(0, count, unroll=count)
        def _(i):
            p = first + stride * i
            score(
                kv.at[0], kv.at[1], win.at[p, 0], win.at[p, 1],
                expon.at[p], dprob.at[p], summit.at[p], lone_out.at[p],
            )

            @pl.when(p != REACH)
            def _():
                stat_copy(p).start()

    def lone_combine():
        parts = []
        for p in range(SPAN):
            if p != REACH:
                stat_copy(2 * REACH - p).wait_recv()
            source = lone_out if p == REACH else lone_in
            parts.append(
                (source[p, 0:thirds, :] + bias[0, p], source[p, thirds : 2 * thirds, :])
            )
        pair = merge(parts)
        put(res_out, pair)
        put(res_in.at[REACH], pair)
        for p in range(SPAN):
            if p != REACH:
                res_copy(p).start()

    def lone_gradients():
        turned = kv[0].T

        def body(p, carry):
            @pl.when(p != REACH)
            def _():
                res_copy(2 * REACH - p).wait_recv()

            dk, dv, dq = gradients(
                expon.at[p], dprob.at[p], summit.at[p], bias[1, p], res_in.at[p],
                win.at[p, 0], win.at[p, 1], turned,
            )
            part[p] = dq
            return carry[0] + dk, carry[1] + dv

        start = (jnp.zeros((tile, DH), jnp.float32), jnp.zeros((tile, DH), jnp.float32))
        dk, dv = lax.fori_loop(0, SPAN, body, start, unroll=SPAN)
        for direction, p in ((0, 0), (1, 2 * REACH)):
            hop_out[direction, 0] = part[p].astype(jnp.bfloat16)
            hop(direction, 0).start()
        block_k[last] = (dk * scale).astype(jnp.bfloat16)
        block_v[last] = dv.astype(jnp.bfloat16)
        spread(1, last)
        spread(2, last)

    def pass_on(distance):
        for direction, p in ((0, distance), (1, 2 * REACH - distance)):
            hop(direction, distance - 1).wait_recv()
            hop_out[direction, distance] = (
                part[p] + hop_in[direction, distance - 1].astype(jnp.float32)
            ).astype(jnp.bfloat16)
            hop(direction, distance).start()

    def lone_finish():
        total = part[REACH]
        for direction in range(2):
            hop(direction, REACH - 1).wait_recv()
            total = total + hop_in[direction, REACH - 1].astype(jnp.float32)
        block_q[last] = (total * scale).T.astype(jnp.bfloat16)
        spread(0, last)

    def received(r):
        return lax.rem(zl - r + RUN, RUN)

    def take_tiles(r):
        newest = received(r)
        for j in QUERY_SIDE:
            in_wait(newest, j)

        @pl.when(newest < REACH)
        def _():
            side_copy(0, newest).start()

        @pl.when(newest >= RUN - REACH)
        def _():
            side_copy(1, newest).start()

    def wait_sides():
        for k in range(REACH):
            side_copy(0, k).wait_recv()
            side_copy(1, k + 1).wait_recv()

    def take_keys(first, count):
        @pl.loop(first, first + count)
        def _(r):
            newest = received(r)
            for j in KEY_SIDE:
                in_wait(newest, j)

            @pl.loop(0, SPAN, unroll=SPAN)
            def _(o):
                wide_score(newest, newest + o)

    def send_stats():
        for p in range(WIDE):
            put(part_stat.at[p], merge(local_parts(p)))
        for side in range(2):
            for what in range(3):
                wstat_copy(side, what).start()

    def wide_combine():
        for side in range(2):
            for what in range(3):
                wstat_copy(side, what).wait_recv()

        def read(ref, *index):
            return (
                ref[(*index, slice(0, thirds), slice(None))],
                ref[(*index, slice(thirds, 2 * thirds), slice(None))],
            )

        for p in range(WIDE):
            parts = [read(part_stat, p)]
            a = p - REACH
            if a < 0:
                parts.append(read(own_stat, 0, a + RUN))
                if a + RUN < REACH:
                    parts.append(read(far_stat, 0, a + RUN))
            elif a >= RUN:
                parts.append(read(own_stat, 1, a - RUN))
                if a - RUN >= RUN - REACH:
                    parts.append(read(far_stat, 1, a - RUN - (RUN - REACH)))
            else:
                if a < REACH:
                    parts.append(read(edge_stat, 0, a))
                if a >= RUN - REACH:
                    parts.append(read(edge_stat, 1, a - (RUN - REACH)))
            put(wres.at[p], merge(parts))

    def home_round(kind, r):
        h = received(r)
        arrived(kind, h)
        spread(kind, h)

    def wide_round(r):
        wide_gradients(lax.rem(zl + r, RUN))

    def finish_queries():
        for side in range(2):
            edge_copy(side).wait_recv()
        for a in range(RUN):
            total = wdq[REACH + a]
            if a < REACH:
                total = total + edge_in[0, a].astype(jnp.float32)
            if a >= RUN - REACH:
                total = total + edge_in[1, a - (RUN - REACH)].astype(jnp.float32)
            made[0, a] = (total * scale).T.astype(jnp.bfloat16)
        for r in range(RUN):
            go_home(0, lax.rem(zl + r, RUN))

    for copy in loads:
        copy.wait()
    send_in(0, QUERY_SIDE)
    send_in(1, QUERY_SIDE)
    for direction in range(2):
        relay(direction, 0).start()
    send_in(2, QUERY_SIDE)
    send_in(3, QUERY_SIDE)
    wdq[...] = jnp.zeros_like(wdq)
    for p in range(SPAN):
        other = lax.rem(me + p - REACH + n_ctx, n_ctx)
        bias[0, p] = listed(me, other)
        bias[1, p] = listed(other, me)
    for i in range(RUN):
        for o in range(SPAN):
            query_tile = lax.rem(first_tile + i + o - REACH + n_ctx, n_ctx)
            wide_bias[i, o] = listed(query_tile, first_tile + i)
    take_tiles(0)
    take_tiles(1)
    forward(1)
    send_in(0, KEY_SIDE)
    send_in(1, KEY_SIDE)
    send_in(2, KEY_SIDE)
    send_in(3, KEY_SIDE)
    lone_score(REACH - 1, 1, 3)
    take_tiles(2)
    take_tiles(3)
    forward(2)
    lone_score(REACH - 2, 4, 2)
    wait_sides()
    take_keys(0, 1)
    take_keys(1, 1)
    take_keys(2, 1)
    take_keys(3, 1)
    send_stats()
    forward(3)
    lone_score(0, SPAN - 1, 2)
    wide_combine()
    wide_round(0)
    lone_combine()
    wide_round(1)
    wide_round(2)
    lone_gradients()
    wide_round(3)
    send_edge(0)
    send_edge(1)
    home_round(1, 0)
    home_round(2, 0)
    pass_on(1)
    home_round(1, 1)
    home_round(2, 1)
    finish_queries()
    pass_on(2)
    home_round(1, 2)
    home_round(2, 2)
    home_round(1, 3)
    home_round(2, 3)
    home_round(0, 0)
    home_round(0, 1)
    home_round(0, 2)
    home_round(0, 3)
    lone_finish()

    for r in range(RUN):
        for j in range(4):
            if r > 0:
                in_copy(r, j).wait_send()
            else:
                @pl.when(jnp.logical_not(stays))
                def _():
                    in_copy(0, j).wait_send()
    for side in range(2):
        for a in range(REACH):
            side_copy(side, a + side).wait_send()
        for what in range(3):
            wstat_copy(side, what).wait_send()
        edge_copy(side).wait_send()
    for kind in range(3):
        for i in range(RUN):
            @pl.when(jnp.logical_not(jnp.logical_and(stays, zl == i)))
            def _():
                home_copy(kind, i).wait_send()
    for direction in range(2):
        for distance in range(REACH):
            relay(direction, distance).wait_send()
            hop(direction, distance).wait_send()
    for p in range(SPAN):
        if p != REACH:
            stat_copy(p).wait_send()
            res_copy(p).wait_send()
    for kind, target in enumerate(targets):
        for h in range(heads):
            own_part(kind, h).wait()
        others = target.at[0, :, pl.ds(0, (n_head - 1) * heads * DH)]
        pltpu.make_async_copy(others, others, out_send.at[kind]).wait()
        pltpu.make_async_copy(others, others, out_recv.at[kind]).wait()


def copy_kernel(a, b, c, a_out, b_out, c_out, sems):
    copies = [
        pltpu.make_async_copy(source, target, sems.at[i])
        for i, (source, target) in enumerate(((a, a_out), (b, b_out), (c, c_out)))
    ]
    for copy in copies:
        copy.start()
    for copy in copies:
        copy.wait()


def shards(queries, keys, values, grad_out, key_tiles, tile_slot):
    tile, width = queries.shape
    heads = width // DH
    n_ctx = lax.axis_size("ctx")
    n_head = lax.axis_size("head")
    rows = tile // n_head
    lines = 2 * (tile // 128)
    bf16, f32 = jnp.bfloat16, jnp.float32
    dma, vmem, smem = pltpu.SemaphoreType.DMA, pltpu.VMEM, pltpu.SMEM
    out = jax.ShapeDtypeStruct((1, rows, n_head * width), bf16)
    pairs = heads * SPAN * tile * tile
    grads = pl.pallas_call(
        functools.partial(kernel, n_ctx, n_head, heads, tile),
        out_shape=(out, out, out),
        in_specs=[pl.BlockSpec(memory_space=pl.ANY)] * 5,
        out_specs=tuple([pl.BlockSpec(memory_space=pltpu.VMEM)] * 3),
        scratch_shapes=[
            smem(key_tiles.shape[::-1], jnp.int32),
            smem((2, SPAN), f32),
            smem((RUN, SPAN), f32),
            vmem((WIDE, 2, tile, DH), bf16),
            vmem((RUN, 2, tile, DH), bf16),
            vmem((RUN, SPAN, tile, tile), f32),
            vmem((RUN, SPAN, tile, tile), f32),
            vmem((RUN, SPAN, 1, tile), f32),
            vmem((RUN, SPAN, lines, 128), f32),
            vmem((WIDE, lines, 128), f32),
            vmem((2, REACH, lines, 128), f32),
            vmem((2, RUN, lines, 128), f32),
            vmem((2, REACH, lines, 128), f32),
            vmem((WIDE, lines, 128), f32),
            vmem((WIDE, DH, tile), f32),
            vmem((2, REACH, DH, tile), bf16),
            vmem((2, REACH, DH, tile), bf16),
            vmem((3, RUN, tile, DH), bf16),
            vmem((SPAN, 2, tile, DH), bf16),
            vmem((2, tile, DH), bf16),
            vmem((SPAN, tile, tile), f32),
            vmem((SPAN, tile, tile), f32),
            vmem((SPAN, 1, tile), f32),
            vmem((SPAN, lines, 128), f32),
            vmem((SPAN, lines, 128), f32),
            vmem((lines, 128), f32),
            vmem((SPAN, lines, 128), f32),
            vmem((SPAN, DH, tile), f32),
            vmem((2, REACH, DH, tile), bf16),
            vmem((2, REACH, DH, tile), bf16),
            vmem((heads, tile, DH), bf16),
            vmem((heads, tile, DH), bf16),
            vmem((heads, tile, DH), bf16),
            dma,
            dma((4,)),
            dma((RUN, 4)),
            dma((RUN, 4)),
            dma((2, REACH)),
            dma((2, REACH)),
            dma((2, 3)),
            dma((2, 3)),
            dma((2,)),
            dma((2,)),
            dma((3, RUN)),
            dma((3, RUN)),
            dma((2, REACH)),
            dma((2, REACH)),
            dma((SPAN,)),
            dma((SPAN,)),
            dma((SPAN,)),
            dma((SPAN,)),
            dma((2, REACH)),
            dma((2, REACH)),
            dma((3,)),
            dma((3,)),
            dma((3, heads)),
        ],
        compiler_params=pltpu.CompilerParams(
            collective_id=0, has_side_effects=True, vmem_limit_bytes=62 * 1024 * 1024
        ),
        cost_estimate=pl.CostEstimate(
            flops=10 * pairs * DH, bytes_accessed=8 * tile * width * 2, transcendentals=pairs
        ),
    )(key_tiles.T, queries, keys, values, grad_out)
    return pl.pallas_call(
        copy_kernel,
        out_shape=(out, out, out),
        in_specs=[pl.BlockSpec(memory_space=pltpu.VMEM)] * 3,
        out_specs=tuple([pl.BlockSpec(memory_space=pl.ANY)] * 3),
        scratch_shapes=[dma((3,))],
    )(*grads)


def solution(mesh):
    in_specs = (P("ctx", "head"), P("ctx", "head"), P("ctx", "head"), P("ctx", "head"), P(), P())
    out_specs = (P("ctx", "head", None), P("ctx", "head", None), P("ctx", "head", None))
    return jax.shard_map(shards, mesh=mesh, in_specs=in_specs, out_specs=out_specs, check_vma=False)
```

```python
import functools
import math

import jax
import jax.numpy as jnp
from jax import lax
from jax.experimental import pallas as pl
from jax.experimental.pallas import tpu as pltpu
from jax.sharding import PartitionSpec as P

DH = 128
REACH = 3
SPAN = 2 * REACH + 1
LOW = -1e30
MESH = pl.DeviceIdType.MESH
NT = (((1,), (1,)), ((), ()))
QUERY_SIDE, KEY_SIDE = (0, 1), (2, 3)
RING = 8
RUN = RING // 2
WIDE = RUN + 2 * REACH


def kernel(
    n_ctx, n_head, heads, tile,
    tiles_hbm, q_hbm, k_hbm, v_hbm, g_hbm,
    dq_out, dk_out, dv_out,
    tiles_ref, bias, wide_bias,
    wwin, wkv, wexp, wdp, wtop, wstat, part_stat, edge_stat, own_stat, far_stat, wres, wdq, edge_out, edge_in, made,
    win, kv, expon, dprob, summit, lone_out, lone_in, res_out, res_in, part, hop_out, hop_in,
    block_q, block_k, block_v,
    tiles_sem, load_sem, in_send, in_recv, side_send, side_recv, wstat_send, wstat_recv,
    edge_send, edge_recv, home_send, home_recv,
    win_send, win_recv, stat_send, stat_recv, res_send, res_recv, hop_send, hop_recv,
    out_send, out_recv, own_sem,
):
    me = lax.axis_index("ctx")
    lane = lax.axis_index("head")
    rows = tile // n_head
    thirds = tile // 128
    scale = DH ** -0.5
    log_scale = scale * math.log2(math.e)
    last = heads - 1
    core = lax.rem(lane, 2)
    z = lax.rem(me, RING)
    zl = lax.rem(z, RUN)
    zh = z // RUN
    chip_lane = lane - core
    line = me - z
    first_tile = RUN * (2 * (me // RING) + core)
    stays = zh == core

    def peer(i):
        return (chip_lane + zh, line + RUN * core + i)

    sides = (
        (chip_lane + 1 - core, lax.rem(me - (1 - core) * RING + n_ctx, n_ctx)),
        (chip_lane + 1 - core, lax.rem(me + core * RING, n_ctx)),
    )

    far_sides = (
        (lane, lax.rem(me - RING + n_ctx, n_ctx)),
        (lane, lax.rem(me + RING, n_ctx)),
    )

    def at(offset):
        return (lane, lax.rem(me + offset + n_ctx, n_ctx))

    def lane_at(shift):
        return (lax.rem(lane + shift, n_head), me)

    tiles_copy = pltpu.make_async_copy(tiles_hbm, tiles_ref, tiles_sem)
    tiles_copy.start()

    barrier = pltpu.get_barrier_semaphore()

    def greet(device):
        pl.semaphore_signal(barrier, inc=1, device_id=device, device_id_type=MESH)

    for i in range(RUN):
        @pl.when(jnp.logical_not(jnp.logical_and(stays, zl == i)))
        def _():
            greet(peer(i))
    for device in sides + far_sides:
        greet(device)
    for offset in range(-REACH, REACH + 1):
        if offset != 0:
            greet(at(offset))
    for shift in range(1, n_head):
        greet(lane_at(shift))

    def columns(h):
        return pl.ds(pl.multiple_of(h * DH, DH), DH)

    loads = [
        pltpu.make_async_copy(source.at[:, columns(last)], target, load_sem.at[i])
        for i, (source, target) in enumerate((
            (q_hbm, win.at[REACH, 0]), (g_hbm, win.at[REACH, 1]),
            (k_hbm, kv.at[0]), (v_hbm, kv.at[1]),
        ))
    ]
    for copy in loads:
        copy.start()

    def landing(a, j):
        return wwin.at[REACH + a, j] if j < 2 else wkv.at[a, j - 2]

    sources = (q_hbm, g_hbm, k_hbm, v_hbm)

    def in_copy(r, j):
        i = lax.rem(zl + r, RUN)
        return pltpu.make_async_remote_copy(
            src_ref=sources[j].at[:, columns(i)],
            dst_ref=landing(zl, j),
            send_sem=in_send.at[r, j],
            recv_sem=in_recv.at[zl, j],
            device_id=peer(i),
            device_id_type=MESH,
        )

    def in_wait(a, j):
        pltpu.make_async_remote_copy(
            src_ref=sources[j].at[:, columns(a)],
            dst_ref=landing(a, j),
            send_sem=in_send.at[0, j],
            recv_sem=in_recv.at[a, j],
            device_id=peer(a),
            device_id_type=MESH,
        ).wait_recv()

    tiles_copy.wait()

    def listed(query_tile, key_tile):
        found = jnp.zeros((), jnp.bool_)
        for j in range(tiles_ref.shape[0]):
            found = jnp.logical_or(found, tiles_ref[j, query_tile] == key_tile)
        return jnp.where(found, 0.0, LOW)

    pl.semaphore_wait(
        barrier, 4 + 2 * REACH + n_head - 1 + RUN - jnp.where(stays, 1, 0).astype(jnp.int32)
    )

    def send_in(r, pair):
        for j in pair:
            if r > 0:
                in_copy(r, j).start()
            else:
                @pl.when(stays)
                def _():
                    pltpu.make_async_copy(
                        sources[j].at[:, columns(zl)], landing(zl, j), in_recv.at[zl, j]
                    ).start()

                @pl.when(jnp.logical_not(stays))
                def _():
                    in_copy(0, j).start()

    def relay(direction, distance):
        step = -1 if direction == 0 else 1
        source = REACH + step * distance
        return pltpu.make_async_remote_copy(
            src_ref=win.at[source],
            dst_ref=win.at[source + step],
            send_sem=win_send.at[direction, distance],
            recv_sem=win_recv.at[direction, distance],
            device_id=at(-step),
            device_id_type=MESH,
        )

    def forward(distance):
        for direction in range(2):
            relay(direction, distance - 1).wait_recv()
            if distance < REACH:
                relay(direction, distance).start()

    def hop(direction, distance):
        return pltpu.make_async_remote_copy(
            src_ref=hop_out.at[direction, distance],
            dst_ref=hop_in.at[direction, distance],
            send_sem=hop_send.at[direction, distance],
            recv_sem=hop_recv.at[direction, distance],
            device_id=at(-1 if direction == 0 else 1),
            device_id_type=MESH,
        )

    def stat_copy(p):
        return pltpu.make_async_remote_copy(
            src_ref=lone_out.at[p],
            dst_ref=lone_in.at[2 * REACH - p],
            send_sem=stat_send.at[p],
            recv_sem=stat_recv.at[2 * REACH - p],
            device_id=at(p - REACH),
            device_id_type=MESH,
        )

    def res_copy(p):
        return pltpu.make_async_remote_copy(
            src_ref=res_out,
            dst_ref=res_in.at[2 * REACH - p],
            send_sem=res_send.at[p],
            recv_sem=res_recv.at[2 * REACH - p],
            device_id=at(p - REACH),
            device_id_type=MESH,
        )

    def side_copy(side, a):
        shift = RUN if side == 0 else -RUN
        slot = a if side == 0 else a - 1
        return pltpu.make_async_remote_copy(
            src_ref=wwin.at[REACH + a],
            dst_ref=wwin.at[REACH + a + shift],
            send_sem=side_send.at[side, slot],
            recv_sem=side_recv.at[side, slot],
            device_id=sides[side],
            device_id_type=MESH,
        )

    def wstat_copy(side, what):
        first, count, inbox, device = (
            (WIDE - REACH if side else 0, REACH, edge_stat, sides[side]),
            (REACH, RUN, own_stat, sides[side]),
            (WIDE - REACH if side else 0, REACH, far_stat, far_sides[side]),
        )[what]
        return pltpu.make_async_remote_copy(
            src_ref=part_stat.at[pl.ds(first, count)],
            dst_ref=inbox.at[1 - side],
            send_sem=wstat_send.at[side, what],
            recv_sem=wstat_recv.at[1 - side, what],
            device_id=device,
            device_id_type=MESH,
        )

    def edge_copy(side):
        return pltpu.make_async_remote_copy(
            src_ref=edge_out.at[side],
            dst_ref=edge_in.at[1 - side],
            send_sem=edge_send.at[side],
            recv_sem=edge_recv.at[1 - side],
            device_id=sides[side],
            device_id_type=MESH,
        )

    blocks = (block_q, block_k, block_v)
    targets = (dq_out, dk_out, dv_out)

    def home_copy(kind, i):
        return pltpu.make_async_remote_copy(
            src_ref=made.at[kind, i],
            dst_ref=blocks[kind].at[zl],
            send_sem=home_send.at[kind, i],
            recv_sem=home_recv.at[kind, zl],
            device_id=peer(i),
            device_id_type=MESH,
        )

    def home_local(kind, i):
        return pltpu.make_async_copy(
            made.at[kind, i], blocks[kind].at[zl], home_recv.at[kind, zl]
        )

    def go_home(kind, i):
        mine = jnp.logical_and(stays, zl == i)

        @pl.when(mine)
        def _():
            home_local(kind, i).start()

        @pl.when(jnp.logical_not(mine))
        def _():
            home_copy(kind, i).start()

    def own_part(kind, h):
        return pltpu.make_async_copy(
            blocks[kind].at[h, pl.ds(pl.multiple_of(lane * rows, 16), rows), :],
            targets[kind].at[0, :, columns(lane * heads + h)],
            own_sem.at[kind, h],
        )

    def spread(kind, h):
        own_part(kind, h).start()

        @pl.loop(1, n_head)
        def _(shift):
            device = lane_at(shift)
            pltpu.make_async_remote_copy(
                src_ref=blocks[kind].at[h, pl.ds(pl.multiple_of(device[0] * rows, 16), rows), :],
                dst_ref=targets[kind].at[0, :, columns(lane * heads + h)],
                send_sem=out_send.at[kind],
                recv_sem=out_recv.at[kind],
                device_id=device,
                device_id_type=MESH,
            ).start()

    def arrived(kind, h):
        pltpu.make_async_remote_copy(
            src_ref=made.at[kind, 0],
            dst_ref=blocks[kind].at[h],
            send_sem=home_send.at[kind, 0],
            recv_sem=home_recv.at[kind, h],
            device_id=peer(h),
            device_id_type=MESH,
        ).wait_recv()

    def wide(ref, start):
        return jnp.concatenate([ref[start + j : start + j + 1, :] for j in range(thirds)], axis=1)

    def score(key, value, query, grad, weights_ref, dp_ref, top_ref, stat_ref):
        scores = lax.dot_general(
            key[...], query[...], NT, preferred_element_type=jnp.float32
        ) * log_scale
        top = jnp.max(scores, axis=0, keepdims=True)
        weights = jnp.exp2(scores - top)
        total = jnp.sum(weights, axis=0, keepdims=True)
        dp = lax.dot_general(value[...], grad[...], NT, preferred_element_type=jnp.float32)
        mean = jnp.sum(weights * dp, axis=0, keepdims=True) / total
        weights_ref[...] = weights
        dp_ref[...] = dp
        top_ref[...] = top
        level = top + jnp.log2(total)
        for j in range(thirds):
            stat_ref[j : j + 1, :] = level[:, j * 128 : (j + 1) * 128]
            stat_ref[thirds + j : thirds + j + 1, :] = mean[:, j * 128 : (j + 1) * 128]

    def merge(parts):
        top = functools.reduce(jnp.maximum, [level for level, _ in parts])
        total = jnp.zeros_like(top)
        mean = jnp.zeros_like(top)
        for level, value in parts:
            weight = jnp.exp2(level - top)
            total = total + weight
            mean = mean + weight * value
        return top + jnp.log2(total), mean / total

    def put(ref, pair):
        ref[0:thirds, :] = pair[0]
        ref[thirds : 2 * thirds, :] = pair[1]

    def gradients(weights_ref, dp_ref, top_ref, offset, result, query, grad, turned):
        factor = jnp.exp2(top_ref[...] + offset - wide(result, 0))
        probs = weights_ref[...] * factor
        dscores = (probs * (dp_ref[...] - wide(result, thirds))).astype(jnp.bfloat16)
        dv = jnp.dot(probs.astype(jnp.bfloat16), grad[...], preferred_element_type=jnp.float32)
        dk = jnp.dot(dscores, query[...], preferred_element_type=jnp.float32)
        return dk, dv, jnp.dot(turned, dscores, preferred_element_type=jnp.float32)

    def wide_score(i, p):
        o = p - i
        score(
            wkv.at[i, 0], wkv.at[i, 1], wwin.at[p, 0], wwin.at[p, 1],
            wexp.at[i, o], wdp.at[i, o], wtop.at[i, o], wstat.at[i, o],
        )

    def local_parts(p):
        return [
            (
                wstat[i, p - i, 0:thirds, :] + wide_bias[i, p - i],
                wstat[i, p - i, thirds : 2 * thirds, :],
            )
            for i in range(RUN)
            if 0 <= p - i < SPAN
        ]

    def wide_gradients(i):
        turned = wkv[i, 0].T

        def body(o, carry):
            p = i + o
            dk, dv, dq = gradients(
                wexp.at[i, o], wdp.at[i, o], wtop.at[i, o], wide_bias[i, o], wres.at[p],
                wwin.at[p, 0], wwin.at[p, 1], turned,
            )
            wdq[p] = wdq[p] + dq
            return carry[0] + dk, carry[1] + dv

        start = (jnp.zeros((tile, DH), jnp.float32), jnp.zeros((tile, DH), jnp.float32))
        dk, dv = lax.fori_loop(0, SPAN, body, start, unroll=SPAN)
        made[1, i] = (dk * scale).astype(jnp.bfloat16)
        made[2, i] = dv.astype(jnp.bfloat16)
        go_home(1, i)
        go_home(2, i)

    def send_edge(side):
        for i in range(REACH):
            edge_out[side, i] = wdq[i if side == 0 else REACH + RUN + i].astype(jnp.bfloat16)
        edge_copy(side).start()

    def lone_score(first, stride, count):
        @pl.loop(0, count, unroll=count)
        def _(i):
            p = first + stride * i
            score(
                kv.at[0], kv.at[1], win.at[p, 0], win.at[p, 1],
                expon.at[p], dprob.at[p], summit.at[p], lone_out.at[p],
            )

            @pl.when(p != REACH)
            def _():
                stat_copy(p).start()

    def lone_combine():
        parts = []
        for p in range(SPAN):
            if p != REACH:
                stat_copy(2 * REACH - p).wait_recv()
            source = lone_out if p == REACH else lone_in
            parts.append(
                (source[p, 0:thirds, :] + bias[0, p], source[p, thirds : 2 * thirds, :])
            )
        pair = merge(parts)
        put(res_out, pair)
        put(res_in.at[REACH], pair)
        for p in range(SPAN):
            if p != REACH:
                res_copy(p).start()

    def lone_gradients():
        turned = kv[0].T

        def body(p, carry):
            @pl.when(p != REACH)
            def _():
                res_copy(2 * REACH - p).wait_recv()

            dk, dv, dq = gradients(
                expon.at[p], dprob.at[p], summit.at[p], bias[1, p], res_in.at[p],
                win.at[p, 0], win.at[p, 1], turned,
            )
            part[p] = dq
            return carry[0] + dk, carry[1] + dv

        start = (jnp.zeros((tile, DH), jnp.float32), jnp.zeros((tile, DH), jnp.float32))
        dk, dv = lax.fori_loop(0, SPAN, body, start, unroll=SPAN)
        for direction, p in ((0, 0), (1, 2 * REACH)):
            hop_out[direction, 0] = part[p].astype(jnp.bfloat16)
            hop(direction, 0).start()
        block_k[last] = (dk * scale).astype(jnp.bfloat16)
        block_v[last] = dv.astype(jnp.bfloat16)
        spread(1, last)
        spread(2, last)

    def pass_on(distance):
        for direction, p in ((0, distance), (1, 2 * REACH - distance)):
            hop(direction, distance - 1).wait_recv()
            hop_out[direction, distance] = (
                part[p] + hop_in[direction, distance - 1].astype(jnp.float32)
            ).astype(jnp.bfloat16)
            hop(direction, distance).start()

    def lone_finish():
        total = part[REACH]
        for direction in range(2):
            hop(direction, REACH - 1).wait_recv()
            total = total + hop_in[direction, REACH - 1].astype(jnp.float32)
        block_q[last] = (total * scale).T.astype(jnp.bfloat16)
        spread(0, last)

    def received(r):
        return lax.rem(zl - r + RUN, RUN)

    def take_tiles(r):
        newest = received(r)
        for j in QUERY_SIDE:
            in_wait(newest, j)

        @pl.when(newest < REACH)
        def _():
            side_copy(0, newest).start()

        @pl.when(newest >= RUN - REACH)
        def _():
            side_copy(1, newest).start()

    def wait_sides():
        for k in range(REACH):
            side_copy(0, k).wait_recv()
            side_copy(1, k + 1).wait_recv()

    def take_keys(first, count):
        @pl.loop(first, first + count)
        def _(r):
            newest = received(r)
            for j in KEY_SIDE:
                in_wait(newest, j)

            @pl.loop(0, SPAN, unroll=SPAN)
            def _(o):
                wide_score(newest, newest + o)

    def send_stats():
        for p in range(WIDE):
            put(part_stat.at[p], merge(local_parts(p)))
        for side in range(2):
            for what in range(3):
                wstat_copy(side, what).start()

    def wide_combine():
        for side in range(2):
            for what in range(3):
                wstat_copy(side, what).wait_recv()

        def read(ref, *index):
            return (
                ref[(*index, slice(0, thirds), slice(None))],
                ref[(*index, slice(thirds, 2 * thirds), slice(None))],
            )

        for p in range(WIDE):
            parts = [read(part_stat, p)]
            a = p - REACH
            if a < 0:
                parts.append(read(own_stat, 0, a + RUN))
                if a + RUN < REACH:
                    parts.append(read(far_stat, 0, a + RUN))
            elif a >= RUN:
                parts.append(read(own_stat, 1, a - RUN))
                if a - RUN >= RUN - REACH:
                    parts.append(read(far_stat, 1, a - RUN - (RUN - REACH)))
            else:
                if a < REACH:
                    parts.append(read(edge_stat, 0, a))
                if a >= RUN - REACH:
                    parts.append(read(edge_stat, 1, a - (RUN - REACH)))
            put(wres.at[p], merge(parts))

    def home_round(kind, r):
        h = received(r)
        arrived(kind, h)
        spread(kind, h)

    def wide_round(r):
        wide_gradients(lax.rem(zl + r, RUN))

    def finish_queries():
        for side in range(2):
            edge_copy(side).wait_recv()
        for a in range(RUN):
            total = wdq[REACH + a]
            if a < REACH:
                total = total + edge_in[0, a].astype(jnp.float32)
            if a >= RUN - REACH:
                total = total + edge_in[1, a - (RUN - REACH)].astype(jnp.float32)
            made[0, a] = (total * scale).T.astype(jnp.bfloat16)
        for r in range(RUN):
            go_home(0, lax.rem(zl + r, RUN))

    for copy in loads:
        copy.wait()
    send_in(0, QUERY_SIDE)
    send_in(1, QUERY_SIDE)
    for direction in range(2):
        relay(direction, 0).start()
    send_in(2, QUERY_SIDE)
    send_in(3, QUERY_SIDE)
    wdq[...] = jnp.zeros_like(wdq)
    for p in range(SPAN):
        other = lax.rem(me + p - REACH + n_ctx, n_ctx)
        bias[0, p] = listed(me, other)
        bias[1, p] = listed(other, me)
    for i in range(RUN):
        for o in range(SPAN):
            query_tile = lax.rem(first_tile + i + o - REACH + n_ctx, n_ctx)
            wide_bias[i, o] = listed(query_tile, first_tile + i)
    take_tiles(0)
    take_tiles(1)
    forward(1)
    send_in(0, KEY_SIDE)
    send_in(1, KEY_SIDE)
    send_in(2, KEY_SIDE)
    send_in(3, KEY_SIDE)
    lone_score(REACH - 1, 1, 3)
    take_tiles(2)
    take_tiles(3)
    forward(2)
    lone_score(REACH - 2, 4, 2)
    wait_sides()
    take_keys(0, 1)
    take_keys(1, 1)
    take_keys(2, 1)
    take_keys(3, 1)
    send_stats()
    forward(3)
    lone_score(0, SPAN - 1, 2)
    wide_combine()
    wide_round(0)
    lone_combine()
    wide_round(2)
    wide_round(1)
    lone_gradients()
    wide_round(3)
    send_edge(0)
    send_edge(1)
    pass_on(1)
    home_round(1, 0)
    home_round(2, 0)
    home_round(1, 2)
    home_round(2, 2)
    finish_queries()
    home_round(1, 1)
    home_round(2, 1)
    pass_on(2)
    home_round(1, 3)
    home_round(2, 3)
    home_round(0, 0)
    home_round(0, 1)
    home_round(0, 2)
    home_round(0, 3)
    lone_finish()

    for r in range(RUN):
        for j in range(4):
            if r > 0:
                in_copy(r, j).wait_send()
            else:
                @pl.when(jnp.logical_not(stays))
                def _():
                    in_copy(0, j).wait_send()
    for side in range(2):
        for a in range(REACH):
            side_copy(side, a + side).wait_send()
        for what in range(3):
            wstat_copy(side, what).wait_send()
        edge_copy(side).wait_send()
    for kind in range(3):
        for i in range(RUN):
            @pl.when(jnp.logical_not(jnp.logical_and(stays, zl == i)))
            def _():
                home_copy(kind, i).wait_send()
    for direction in range(2):
        for distance in range(REACH):
            relay(direction, distance).wait_send()
            hop(direction, distance).wait_send()
    for p in range(SPAN):
        if p != REACH:
            stat_copy(p).wait_send()
            res_copy(p).wait_send()
    for kind, target in enumerate(targets):
        for h in range(heads):
            own_part(kind, h).wait()
        others = target.at[0, :, pl.ds(0, (n_head - 1) * heads * DH)]
        pltpu.make_async_copy(others, others, out_send.at[kind]).wait()
        pltpu.make_async_copy(others, others, out_recv.at[kind]).wait()


def copy_kernel(a, b, c, a_out, b_out, c_out, sems):
    copies = [
        pltpu.make_async_copy(source, target, sems.at[i])
        for i, (source, target) in enumerate(((a, a_out), (b, b_out), (c, c_out)))
    ]
    for copy in copies:
        copy.start()
    for copy in copies:
        copy.wait()


def shards(queries, keys, values, grad_out, key_tiles, tile_slot):
    tile, width = queries.shape
    heads = width // DH
    n_ctx = lax.axis_size("ctx")
    n_head = lax.axis_size("head")
    rows = tile // n_head
    lines = 2 * (tile // 128)
    bf16, f32 = jnp.bfloat16, jnp.float32
    dma, vmem, smem = pltpu.SemaphoreType.DMA, pltpu.VMEM, pltpu.SMEM
    out = jax.ShapeDtypeStruct((1, rows, n_head * width), bf16)
    pairs = heads * SPAN * tile * tile
    grads = pl.pallas_call(
        functools.partial(kernel, n_ctx, n_head, heads, tile),
        out_shape=(out, out, out),
        in_specs=[pl.BlockSpec(memory_space=pl.ANY)] * 5,
        out_specs=tuple([pl.BlockSpec(memory_space=pltpu.VMEM)] * 3),
        scratch_shapes=[
            smem(key_tiles.shape[::-1], jnp.int32),
            smem((2, SPAN), f32),
            smem((RUN, SPAN), f32),
            vmem((WIDE, 2, tile, DH), bf16),
            vmem((RUN, 2, tile, DH), bf16),
            vmem((RUN, SPAN, tile, tile), f32),
            vmem((RUN, SPAN, tile, tile), f32),
            vmem((RUN, SPAN, 1, tile), f32),
            vmem((RUN, SPAN, lines, 128), f32),
            vmem((WIDE, lines, 128), f32),
            vmem((2, REACH, lines, 128), f32),
            vmem((2, RUN, lines, 128), f32),
            vmem((2, REACH, lines, 128), f32),
            vmem((WIDE, lines, 128), f32),
            vmem((WIDE, DH, tile), f32),
            vmem((2, REACH, DH, tile), bf16),
            vmem((2, REACH, DH, tile), bf16),
            vmem((3, RUN, tile, DH), bf16),
            vmem((SPAN, 2, tile, DH), bf16),
            vmem((2, tile, DH), bf16),
            vmem((SPAN, tile, tile), f32),
            vmem((SPAN, tile, tile), f32),
            vmem((SPAN, 1, tile), f32),
            vmem((SPAN, lines, 128), f32),
            vmem((SPAN, lines, 128), f32),
            vmem((lines, 128), f32),
            vmem((SPAN, lines, 128), f32),
            vmem((SPAN, DH, tile), f32),
            vmem((2, REACH, DH, tile), bf16),
            vmem((2, REACH, DH, tile), bf16),
            vmem((heads, tile, DH), bf16),
            vmem((heads, tile, DH), bf16),
            vmem((heads, tile, DH), bf16),
            dma,
            dma((4,)),
            dma((RUN, 4)),
            dma((RUN, 4)),
            dma((2, REACH)),
            dma((2, REACH)),
            dma((2, 3)),
            dma((2, 3)),
            dma((2,)),
            dma((2,)),
            dma((3, RUN)),
            dma((3, RUN)),
            dma((2, REACH)),
            dma((2, REACH)),
            dma((SPAN,)),
            dma((SPAN,)),
            dma((SPAN,)),
            dma((SPAN,)),
            dma((2, REACH)),
            dma((2, REACH)),
            dma((3,)),
            dma((3,)),
            dma((3, heads)),
        ],
        compiler_params=pltpu.CompilerParams(
            collective_id=0, has_side_effects=True, vmem_limit_bytes=62 * 1024 * 1024
        ),
        cost_estimate=pl.CostEstimate(
            flops=10 * pairs * DH, bytes_accessed=8 * tile * width * 2, transcendentals=pairs
        ),
    )(key_tiles.T, queries, keys, values, grad_out)
    return pl.pallas_call(
        copy_kernel,
        out_shape=(out, out, out),
        in_specs=[pl.BlockSpec(memory_space=pltpu.VMEM)] * 3,
        out_specs=tuple([pl.BlockSpec(memory_space=pl.ANY)] * 3),
        scratch_shapes=[dma((3,))],
    )(*grads)


def solution(mesh):
    in_specs = (P("ctx", "head"), P("ctx", "head"), P("ctx", "head"), P("ctx", "head"), P(), P())
    out_specs = (P("ctx", "head", None), P("ctx", "head", None), P("ctx", "head", None))
    return jax.shard_map(shards, mesh=mesh, in_specs=in_specs, out_specs=out_specs, check_vma=False)
```
